32 devices in a mesh: gx: 8 (over y, x, core), gy: 4 (over z).
Axes of the slice: x: 2, y: 2, z: 4, core: 2. Of those that a mesh axis runs over, the one named last changes fastest.
Arguments:
- rhs_field: float32 [3, 16, 128, 128], P(None, 'gx', 'gy'), may hold values from -6 to 6
- shear_modulus: float32 [16, 128, 128], P('gx', 'gy'), may hold values from 0.3 to 3
- lame_lambda: float32 [16, 128, 128], P('gx', 'gy'), may hold values from 0.3 to 3
- group_start: int32 [8, 4], P('gx'), may hold values from 0 to 1, as said below
Outputs:
- solution_field: float32 [3, 16, 128, 128], P(None, 'gx', 'gy')
- residual_field: float32 [3, 16, 128, 128], P(None, 'gx', 'gy')
The draws below stay inside these ranges and needn't reach their ends.
Inputs may be any that keep to these rules, and one draw needn't show every extreme that they name: `group_start`: each index of gx has exactly one 1, at an index of gy from 1 to 3.
All inputs are finite; a program needn't handle non-finite values.
Results may differ from the reference program's by a relative error of at most 0.00011.
Values sent between devices are 32-bit elements; how exact they have to be, the bound alone decides.
A program may use at most 64 MiB of HBM per device.

```python
import math
import jax
import jax.numpy as jnp

CX = 2
CY = 32
SWEEPS = 3
COARSE_SWEEPS = 4
NX = 16
NY = 128
NZ = 128
N_GX = 8
N_GY = 4


def draw_rhs_field(key, part):
    full_shape = (3, NX, NY, NZ)
    return jnp.clip(jax.random.normal(key, full_shape, jnp.float32) + 1.0, -6.0, 6.0)


def draw_group_start(key, part):
    split_at = jax.random.randint(jax.random.fold_in(key, 7), (N_GX, 1), 1, N_GY)
    return jnp.where(jnp.arange(N_GY, dtype=jnp.int32)[None, :] == split_at, 1, 0).astype(jnp.int32)


def block_levels(stream_key, shape, shards, low, high):
    loudness, own = 1.0, jax.random.fold_in(stream_key, 6)
    for position, parts in shards:
        heights = jnp.exp(jax.random.uniform(jax.random.fold_in(own, position), (parts,), jnp.float32, low / len(shards), high / len(shards)))
        loudness = loudness * jnp.repeat(heights, shape[position] // parts).reshape([-1 if axis == position else 1 for axis in range(len(shape))])
    return loudness


def setup_inputs(seed: int = 0) -> dict:
    arg_keys = jax.random.split(jax.random.key(seed), 5)
    rhs_field = draw_rhs_field(jax.random.fold_in(arg_keys[4], 71), 0)
    shear_modulus = jnp.clip(jnp.exp(math.log(3.0) - 2.3025851 * jax.random.uniform(arg_keys[1], (NX, NY, NZ), jnp.float32) ** block_levels(arg_keys[1], (NX, NY, NZ), ((0, 8), (1, 4)), -0.2, 0.2)), 0.3, 3.0)
    lame_lambda = jnp.clip(jnp.exp(math.log(3.0) - 2.3025851 * jax.random.uniform(arg_keys[2], (NX, NY, NZ), jnp.float32) ** block_levels(arg_keys[2], (NX, NY, NZ), ((0, 8), (1, 4)), -0.2, 0.2)), 0.3, 3.0)
    group_start = draw_group_start(jax.random.fold_in(arg_keys[4], 71), 0)
    return dict(rhs_field=rhs_field, shear_modulus=shear_modulus, lame_lambda=lame_lambda, group_start=group_start)


LOW_BOUND = 0.5
HIGH_BOUND = 6.0
SHIFT_SCALE = 48.0
UNITS = ((1, 0, 0), (0, 1, 0), (0, 0, 1))


def shifted(array, step_x, step_y, step_z):
    size_x = array.shape[-3] - 2
    size_y = array.shape[-2] - 2
    size_z = array.shape[-1] - 2
    return array[..., 1 + step_x:1 + step_x + size_x, 1 + step_y:1 + step_y + size_y, 1 + step_z:1 + step_z + size_z]


def diagonal(mu_pad, lam_pad, scale):
    mu_centre = shifted(mu_pad, 0, 0, 0)
    lam_centre = shifted(lam_pad, 0, 0, 0)
    faces = 0.0
    for unit in UNITS:
        backward = tuple(-value for value in unit)
        faces = faces + 0.5 * (mu_centre + shifted(mu_pad, *unit)) + 0.5 * (mu_centre + shifted(mu_pad, *backward))
    results = []
    for unit in UNITS:
        backward = tuple(-value for value in unit)
        results.append(scale * (faces + lam_centre + shifted(lam_pad, *backward)))
    return jnp.stack(results)


def operate(field_pad, mu_pad, lam_pad, scale):
    mu_centre = shifted(mu_pad, 0, 0, 0)
    lam_centre = shifted(lam_pad, 0, 0, 0)
    components = [field_pad[0], field_pad[1], field_pad[2]]
    centres = [shifted(value, 0, 0, 0) for value in components]
    laplace = [0.0, 0.0, 0.0]
    for unit in UNITS:
        backward = tuple(-value for value in unit)
        face_up = 0.5 * (mu_centre + shifted(mu_pad, *unit))
        face_down = 0.5 * (mu_centre + shifted(mu_pad, *backward))
        for comp_id in range(3):
            laplace[comp_id] = laplace[comp_id] + face_up * (shifted(components[comp_id], *unit) - centres[comp_id]) - face_down * (centres[comp_id] - shifted(components[comp_id], *backward))

    def spread(offset):
        total = 0.0
        for comp_id in range(3):
            ahead = tuple(offset[axis_id] + UNITS[comp_id][axis_id] for axis_id in range(3))
            total = total + (shifted(components[comp_id], *ahead) - shifted(components[comp_id], *offset))
        return total

    stress_here = lam_centre * spread((0, 0, 0))
    results = []
    for comp_id in range(3):
        backward = tuple(-value for value in UNITS[comp_id])
        grad_term = stress_here - shifted(lam_pad, *backward) * spread(backward)
        results.append(scale * (-laplace[comp_id] - grad_term))
    return jnp.stack(results)


def smooth(solution, residual, inverse_diag, apply_fn, steps):
    midpoint = 0.5 * (HIGH_BOUND + LOW_BOUND)
    halfwidth = 0.5 * (HIGH_BOUND - LOW_BOUND)
    sharpness = midpoint / halfwidth
    weight_old = 1.0 / sharpness
    direction = inverse_diag * residual / midpoint
    solution = solution + direction
    residual = residual - apply_fn(direction)
    for step_id in range(steps - 1):
        weight_new = 1.0 / (2.0 * sharpness - weight_old)
        direction = weight_new * weight_old * direction + (2.0 * weight_new / halfwidth) * (inverse_diag * residual)
        solution = solution + direction
        residual = residual - apply_fn(direction)
        weight_old = weight_new
    return solution, residual


def pad_groups(array, starts):
    cont = jnp.where(starts[..., 1:] == 0, 1.0, 0.0)
    closed = jnp.zeros_like(cont[..., :1])
    lower = jnp.concatenate([closed, cont], axis=-1)[..., None, None, None]
    upper = jnp.concatenate([cont, closed], axis=-1)[..., None, None, None]
    below = jnp.concatenate([jnp.zeros_like(array[..., :1, :, :1, :]), array[..., :-1, :, -1:, :]], axis=-4) * lower
    above = jnp.concatenate([array[..., 1:, :, :1, :], jnp.zeros_like(array[..., :1, :, :1, :])], axis=-4) * upper
    joined = jnp.concatenate([below, array, above], axis=-2)
    widths = [(0, 0)] * (joined.ndim - 3) + [(1, 1), (0, 0), (1, 1)]
    return jnp.pad(joined, widths)


def same_group(starts):
    count = starts.shape[-1]
    marks = jnp.where(jnp.arange(count, dtype=jnp.int32) > 0, starts, 0).astype(jnp.int32)
    labels = jnp.cumsum(marks, axis=-1).astype(jnp.int32)
    return jnp.where(labels[..., :, None] == labels[..., None, :], 1.0, 0.0).astype(jnp.float32)


def reference(rhs_field, shear_modulus, lame_lambda, group_start):
    mu_pad = jnp.pad(shear_modulus, 1)
    lam_pad = jnp.pad(lame_lambda, 1)
    inverse_diag = 1.0 / diagonal(mu_pad, lam_pad, 1.0)

    def fine_apply(field):
        return operate(jnp.pad(field, ((0, 0), (1, 1), (1, 1), (1, 1))), mu_pad, lam_pad, 1.0)

    solution, residual = smooth(jnp.zeros_like(rhs_field), rhs_field, inverse_diag, fine_apply, SWEEPS)
    coarse_res = residual.reshape(3, NX // 2, 2, NY // 2, 2, NZ // 2, 2).sum(axis=(2, 4, 6))
    coarse_mu = shear_modulus.reshape(NX // 2, 2, NY // 2, 2, NZ // 2, 2).mean(axis=(1, 3, 5))
    coarse_lam = lame_lambda.reshape(NX // 2, 2, NY // 2, 2, NZ // 2, 2).mean(axis=(1, 3, 5))

    def to_blocks(array):
        return array.reshape(array.shape[0], N_GX, CX // 2, N_GY, CY // 2, NZ // 2).transpose(0, 1, 3, 2, 4, 5)

    res_blocks = to_blocks(coarse_res)
    coef_pad = pad_groups(to_blocks(jnp.stack([coarse_mu, coarse_lam])), group_start)
    coarse_inverse = 1.0 / diagonal(coef_pad[0], coef_pad[1], 4.0)

    def coarse_apply(field):
        return operate(pad_groups(field, group_start), coef_pad[0], coef_pad[1], 4.0)

    correction, coarse_left = smooth(jnp.zeros_like(res_blocks), res_blocks, coarse_inverse, coarse_apply, COARSE_SWEEPS)
    device_sums = res_blocks.sum(axis=(3, 4, 5))
    members = same_group(group_start)
    totals = jnp.einsum("gij,cgj->cgi", members, device_sums)
    cells_dev = (CX // 2) * (CY // 2) * (NZ // 2)
    group_cells = members.sum(axis=-1) * cells_dev
    group_shift = totals / (SHIFT_SCALE * group_cells[None])
    correction = correction + group_shift[:, :, :, None, None, None]
    correction = correction.transpose(0, 1, 3, 2, 4, 5).reshape(3, NX // 2, NY // 2, NZ // 2)
    fine_corr = jnp.broadcast_to(correction[:, :, None, :, None, :, None], (3, NX // 2, 2, NY // 2, 2, NZ // 2, 2)).reshape(3, NX, NY, NZ)
    solution = solution + fine_corr
    residual = residual - fine_apply(fine_corr)
    solution, residual = smooth(solution, residual, inverse_diag, fine_apply, SWEEPS)
    return solution, residual
```

```python
import functools

import jax
import jax.numpy as jnp
from jax import lax
from jax.experimental import pallas as pl
from jax.experimental.pallas import tpu as pltpu
from jax.sharding import PartitionSpec as P

SWEEPS = 3
COARSE_SWEEPS = 4
LOW_BOUND = 0.5
HIGH_BOUND = 6.0
SHIFT_SCALE = 48.0

MID = 0.5 * (HIGH_BOUND + LOW_BOUND)
HALF = 0.5 * (HIGH_BOUND - LOW_BOUND)
SIGMA = MID / HALF

H = 8
DIRS = ((1, 0), (-1, 0), (0, 1), (0, -1), (1, -1), (-1, 1), (1, 1), (-1, -1))


def weights(steps):
    out = [(0.0, 1.0 / MID)]
    old = 1.0 / SIGMA
    for _ in range(steps - 1):
        new = 1.0 / (2.0 * SIGMA - old)
        out.append((new * old, 2.0 * new / HALF))
        old = new
    return out


def kernel(
    n_gx, n_gy, rhs_ref, mu_ref, lam_ref, starts_ref, sol_ref, res_ref,
    coef, rhs, inv, dirs, rbuf, r2buf, fc, sums, send, recv, sum_send, sum_recv,
):
    rows = rhs_ref.shape[2]
    lanes = rhs_ref.shape[3]
    ext = rows + 2 * H
    gx = lax.axis_index("gx")
    gy = lax.axis_index("gy")
    own = slice(H, H + rows)

    def exists(sx, sy):
        ok = None
        for pos, step, count in ((gx, sx, n_gx), (gy, sy, n_gy)):
            if step == 1:
                here = pos < count - 1
            elif step == -1:
                here = pos > 0
            else:
                continue
            ok = here if ok is None else jnp.logical_and(ok, here)
        return ok

    coef[0, 2:4, own, :] = mu_ref[...]
    coef[1, 2:4, own, :] = lam_ref[...]
    rhs[:, 1:3, own, :] = rhs_ref[...]

    def clear(ref, index):
        ref[index] = jnp.zeros_like(ref[index])

    every = slice(None)
    for edge, planes2, planes1, planef in (
        (gx == 0, slice(0, 2), 0, 0),
        (gx == n_gx - 1, slice(4, 6), 3, 2),
    ):

        @pl.when(edge)
        def _(planes2=planes2, planes1=planes1, planef=planef):
            clear(coef, (every, planes2))
            clear(rhs, (every, planes1))
            clear(rbuf, (every, planes1))
            clear(fc, (every, planef))
            for k in (1, 2, 4, 5):
                clear(dirs, (k, every, planes1))

    for edge, edge_rows in ((gy == 0, slice(0, H)), (gy == n_gy - 1, slice(H + rows, ext))):

        @pl.when(edge)
        def _(edge_rows=edge_rows):
            for ref in (coef, rhs, rbuf, fc):
                clear(ref, (every, every, edge_rows))
            for k in (1, 2, 4, 5):
                clear(dirs, (k, every, every, edge_rows))

    barrier = pltpu.get_barrier_semaphore()
    expected = jnp.int32(n_gy - 1)
    for sx, sy in DIRS:
        if sx == 0:
            continue

        @pl.when(exists(sx, sy))
        def _(sx=sx, sy=sy):
            pl.semaphore_signal(
                barrier, inc=1, device_id=(gx + sx, gy + sy), device_id_type=pl.DeviceIdType.MESH
            )

        expected = expected + exists(sx, sy).astype(jnp.int32)
    for step in range(1, n_gy):
        pl.semaphore_signal(
            barrier,
            inc=1,
            device_id=(gx, lax.rem(gy + step, n_gy)),
            device_id_type=pl.DeviceIdType.MESH,
        )
    pl.semaphore_wait(barrier, expected)

    def message(ref, lead, kind, round_id, way):
        sx, sy = DIRS[way]
        if kind == "coef":
            src_p = slice(2, 4)
            dst_p = {0: slice(2, 4), 1: slice(0, 2), -1: slice(4, 6)}[sx]
        elif kind == "fine":
            src_p = {0: slice(1, 3), 1: slice(2, 3), -1: slice(1, 2)}[sx]
            dst_p = {0: slice(1, 3), 1: slice(0, 1), -1: slice(3, 4)}[sx]
        else:
            src_p = slice(1, 2)
            dst_p = {0: slice(1, 2), 1: slice(0, 1), -1: slice(2, 3)}[sx]
        src_r = {0: own, 1: slice(rows, rows + H), -1: slice(H, 2 * H)}[sy]
        dst_r = {0: own, 1: slice(0, H), -1: slice(H + rows, ext)}[sy]
        return pltpu.make_async_remote_copy(
            src_ref=ref.at[lead + (every, src_p, src_r)],
            dst_ref=ref.at[lead + (every, dst_p, dst_r)],
            send_sem=send.at[round_id, way],
            recv_sem=recv.at[round_id, way],
            device_id=(gx + sx, gy + sy),
            device_id_type=pl.DeviceIdType.MESH,
        )

    started = []

    def start(ref, lead, kind, round_id, ways):
        for way in ways:
            started.append((ref, lead, kind, round_id, way))

            @pl.when(exists(*DIRS[way]))
            def _(way=way):
                message(ref, lead, kind, round_id, way).start()

    def arrive(ref, lead, kind, round_id, ways):
        for way in ways:
            sx, sy = DIRS[way]

            @pl.when(exists(-sx, -sy))
            def _(way=way):
                message(ref, lead, kind, round_id, way).wait_recv()

    ALL = range(8)
    STAR = range(6)
    start(coef, (), "coef", 0, ALL)
    start(rhs, (), "fine", 1, ALL)

    def lane_of(count):
        return lax.broadcasted_iota(jnp.int32, (count, lanes), 1)

    def make_zshift(count, dist):
        lane = lane_of(count)

        def up(a):
            return jnp.where(lane >= lanes - dist, 0.0, pltpu.roll(a, lanes - dist, 1))

        def down(a):
            return jnp.where(lane < dist, 0.0, pltpu.roll(a, dist, 1))

        return up, down

    def coef_at(which, plane, first, count):
        return coef[which, plane, first : first + count, :]

    def operate(load, plane, first, count):
        up, down = make_zshift(count, 1)

        def mu(dp, dy):
            return coef_at(0, plane + 1 + dp, first + dy, count)

        def lam(dp, dy):
            return coef_at(1, plane + 1 + dp, first + dy, count)

        m0 = mu(0, 0)
        faces = [
            0.5 * (m0 + mu(1, 0)),
            0.5 * (m0 + mu(-1, 0)),
            0.5 * (m0 + mu(0, 1)),
            0.5 * (m0 + mu(0, -1)),
            0.5 * (m0 + up(m0)),
            0.5 * (m0 + down(m0)),
        ]
        centre = [load(c, plane, 0, 0) for c in range(3)]
        vx_up = load(0, plane, 1, 0)
        vy_up = load(1, plane, 0, 1)
        vz_up = up(centre[2])
        here = lam(0, 0) * (
            (vx_up - centre[0]) + (vy_up - centre[1]) + (vz_up - centre[2])
        )
        vx_low = load(0, plane, -1, 0)
        vy_side = load(1, plane, -1, 0)
        vz_side = load(2, plane, -1, 0)
        back_x = lam(-1, 0) * (
            (centre[0] - vx_low)
            + (load(1, plane, -1, 1) - vy_side)
            + (up(vz_side) - vz_side)
        )
        vx_below = load(0, plane, 0, -1)
        vy_low = load(1, plane, 0, -1)
        vz_below = load(2, plane, 0, -1)
        back_y = lam(0, -1) * (
            (load(0, plane, 1, -1) - vx_below)
            + (centre[1] - vy_low)
            + (up(vz_below) - vz_below)
        )
        backs = [back_x, back_y, down(here)]
        out = []
        for c in range(3):
            v = centre[c]
            laplace = (
                faces[0] * ((vx_up if c == 0 else load(c, plane, 1, 0)) - v)
                - faces[1] * (v - load(c, plane, -1, 0))
                + faces[2] * ((vy_up if c == 1 else load(c, plane, 0, 1)) - v)
                - faces[3] * (v - load(c, plane, 0, -1))
                + faces[4] * ((vz_up if c == 2 else up(v)) - v)
                - faces[5] * (v - down(v))
            )
            out.append(-laplace - (here - backs[c]))
        return out

    def direction_load(k, first, count):
        def load(c, plane, dp, dy):
            return dirs[k, c, plane + dp, first + dy : first + dy + count, :]

        return load

    steps = weights(SWEEPS)

    arrive(coef, (), "coef", 0, ALL)
    wide_first, wide = H - 1, rows + 2
    up, down = make_zshift(wide, 1)
    row_id = lax.broadcasted_iota(jnp.int32, (wide, lanes), 0)
    row_ok = jnp.logical_and(
        jnp.logical_or(row_id > 0, gy > 0), jnp.logical_or(row_id < wide - 1, gy < n_gy - 1)
    )
    for plane in range(4):
        m0 = coef_at(0, plane + 1, wide_first, wide)
        l0 = coef_at(1, plane + 1, wide_first, wide)
        total = (
            0.5 * (m0 + coef_at(0, plane + 2, wide_first, wide))
            + 0.5 * (m0 + coef_at(0, plane, wide_first, wide))
            + 0.5 * (m0 + coef_at(0, plane + 1, wide_first + 1, wide))
            + 0.5 * (m0 + coef_at(0, plane + 1, wide_first - 1, wide))
            + 0.5 * (m0 + up(m0))
            + 0.5 * (m0 + down(m0))
            + l0
        )
        sides = (
            coef_at(1, plane, wide_first, wide),
            coef_at(1, plane + 1, wide_first - 1, wide),
            down(l0),
        )
        ok = row_ok
        if plane == 0:
            ok = jnp.logical_and(ok, gx > 0)
        if plane == 3:
            ok = jnp.logical_and(ok, gx < n_gx - 1)
        for c in range(3):
            inv[c, plane, wide_first : wide_first + wide, :] = jnp.where(
                ok, 1.0 / (total + sides[c]), 0.0
            )
    arrive(rhs, (), "fine", 1, ALL)
    wide_rows = slice(wide_first, wide_first + wide)
    for plane in range(4):
        for c in range(3):
            dirs[0, c, plane, wide_rows, :] = (
                steps[0][1] * inv[c, plane, wide_rows, :] * rhs[c, plane, wide_rows, :]
            )

    def relax(k, source, target, following):
        for plane in (1, 2):
            applied = operate(direction_load(k, H, rows), plane, H, rows)
            for c in range(3):
                left = source(c, plane) - applied[c]
                target(c, plane, left)
                if following is not None:
                    dirs[k + 1, c, plane, own, :] = (
                        following[0] * dirs[k, c, plane, own, :]
                        + following[1] * (inv[c, plane, own, :] * left)
                    )

    def into_rbuf(c, plane, value):
        rbuf[c, plane, own, :] = value

    def from_rbuf(c, plane):
        return rbuf[c, plane, own, :]

    relax(0, lambda c, plane: rhs[c, plane, own, :], into_rbuf, steps[1])
    start(dirs, (1,), "fine", 2, STAR)

    lane = lane_of(ext)
    rid = lax.broadcasted_iota(jnp.int32, (ext, lanes), 0)
    lane_even = lane % 2 == 0
    row_even = rid % 2 == 0

    def cube_sum(a):
        a = a + jnp.where(lane_even, pltpu.roll(a, lanes - 1, 1), pltpu.roll(a, 1, 1))
        return a + jnp.where(row_even, pltpu.roll(a, ext - 1, 0), pltpu.roll(a, 1, 0))

    labels = []
    label = jnp.int32(0)
    for j in range(n_gy):
        if j > 0:
            label = label + starts_ref[0, j]
        labels.append(label)
    mine = labels[0]
    before = labels[0] - 1
    after = labels[0] - 1
    for j in range(n_gy):
        mine = jnp.where(gy == j, labels[j], mine)
        if j > 0:
            before = jnp.where(gy == j, labels[j - 1], before)
        if j < n_gy - 1:
            after = jnp.where(gy == j, labels[j + 1], after)
    low_open = jnp.logical_and(gy > 0, before == mine)
    high_open = jnp.logical_and(gy < n_gy - 1, after == mine)
    inside = jnp.logical_and(
        jnp.logical_or(rid >= H, low_open), jnp.logical_or(rid < H + rows, high_open)
    )
    up2, down2 = make_zshift(ext, 2)

    def row_up(a):
        return pltpu.roll(a, ext - 2, 0)

    def row_down(a):
        return pltpu.roll(a, 2, 0)

    cmu = jnp.where(inside, 0.125 * cube_sum(coef[0, 2] + coef[0, 3]), 0.0)
    clam = jnp.where(inside, 0.125 * cube_sum(coef[1, 2] + coef[1, 3]), 0.0)
    cf = [
        0.5 * (cmu + row_up(cmu)),
        0.5 * (cmu + row_down(cmu)),
        0.5 * (cmu + up2(cmu)),
        0.5 * (cmu + down2(cmu)),
    ]
    csum = cmu + cf[0] + cf[1] + cf[2] + cf[3]
    cinv = [
        jnp.where(inside, 1.0 / (4.0 * (csum + clam + side)), 0.0)
        for side in (0.0, row_down(clam), down2(clam))
    ]

    def coarse_operate(v):
        vy_up = row_up(v[1])
        vz_up = up2(v[2])
        here = clam * ((vy_up - v[1]) + (vz_up - v[2]) - v[0])
        backs = [0.0, row_down(here), down2(here)]
        out = []
        for c in range(3):
            laplace = (
                cf[0] * ((vy_up if c == 1 else row_up(v[c])) - v[c])
                - cf[1] * (v[c] - row_down(v[c]))
                + cf[2] * ((vz_up if c == 2 else up2(v[c])) - v[c])
                - cf[3] * (v[c] - down2(v[c]))
                - cmu * v[c]
            )
            out.append(4.0 * (-laplace - (here - backs[c])))
        return out

    for c in range(3):
        for plane in (1, 2):
            sol_ref[c, plane - 1] = dirs[0, c, plane, own, :] + dirs[1, c, plane, own, :]
    arrive(dirs, (1,), "fine", 2, STAR)
    relax(1, from_rbuf, into_rbuf, steps[2])
    start(dirs, (2,), "fine", 3, STAR)
    for c in range(3):
        for plane in (1, 2):
            sol_ref[c, plane - 1] += dirs[2, c, plane, own, :]
    arrive(dirs, (2,), "fine", 3, STAR)
    relax(2, from_rbuf, into_rbuf, None)
    start(rbuf, (), "fine", 4, (2, 3, 0, 1, 4, 5, 6, 7))

    sub = lax.broadcasted_iota(jnp.int32, (8, lanes), 0)
    part = jnp.zeros((8, lanes), jnp.float32)
    for c in range(3):
        both = rbuf[c, 1, own, :] + rbuf[c, 2, own, :]
        part = jnp.where(sub == c, jnp.sum(both, axis=0, keepdims=True), part)
    sums[0] = part

    def sum_message(step):
        return pltpu.make_async_remote_copy(
            src_ref=sums.at[0],
            dst_ref=sums.at[step],
            send_sem=sum_send.at[step],
            recv_sem=sum_recv.at[step],
            device_id=(gx, lax.rem(gy + step, n_gy)),
            device_id_type=pl.DeviceIdType.MESH,
        )

    for step in range(1, n_gy):
        sum_message(step).start()

    arrive(rbuf, (), "fine", 4, (2, 3))
    left = [
        jnp.where(inside, cube_sum(rbuf[c, 1] + rbuf[c, 2]), 0.0) for c in range(3)
    ]
    coarse_steps = weights(COARSE_SWEEPS)
    direction = [coarse_steps[0][1] * cinv[c] * left[c] for c in range(3)]
    smoothed = direction
    for old, new in coarse_steps[1:]:
        applied = coarse_operate(direction)
        left = [left[c] - applied[c] for c in range(3)]
        direction = [old * direction[c] + new * (cinv[c] * left[c]) for c in range(3)]
        smoothed = [smoothed[c] + direction[c] for c in range(3)]

    total = sums[0]
    members = jnp.float32(1.0)
    for step in range(1, n_gy):
        sum_message(step).wait_recv()
        source = lax.rem(gy + n_gy - step, n_gy)
        other = labels[0]
        for j in range(1, n_gy):
            other = jnp.where(source == j, labels[j], other)
        same = jnp.where(other == mine, jnp.float32(1.0), jnp.float32(0.0))
        total = total + same * sums[step]
        members = members + same
    cells_dev = (rows // 2) * (lanes // 2)
    scale = jnp.full((8, 1), SHIFT_SCALE * cells_dev, jnp.float32) * members
    shift = jnp.sum(total, axis=1, keepdims=True) / scale
    for c in range(3):
        fc[c, 1, own, :] = smoothed[c][H : H + rows] + shift[c : c + 1, :]
    start(fc, (), "coarse", 5, ALL)
    for c in range(3):
        for plane in (1, 2):
            sol_ref[c, plane - 1] += fc[c, 1, own, :]
    arrive(rbuf, (), "fine", 4, (0, 1, 4, 5, 6, 7))
    arrive(fc, (), "coarse", 5, ALL)

    def fc_load(c, plane, dp, dy):
        return fc[c, (plane + 1 + dp) // 2, wide_first + dy : wide_first + dy + wide, :]

    for plane in range(4):
        applied = operate(fc_load, plane, wide_first, wide)
        for c in range(3):
            value = rbuf[c, plane, wide_rows, :] - applied[c]
            r2buf[c, plane, wide_rows, :] = value
            dirs[3, c, plane, wide_rows, :] = steps[0][1] * inv[c, plane, wide_rows, :] * value

    def into_r2(c, plane, value):
        r2buf[c, plane, own, :] = value

    def from_r2(c, plane):
        return r2buf[c, plane, own, :]

    def into_result(c, plane, value):
        res_ref[c, plane - 1] = value

    relax(3, from_r2, into_r2, steps[1])
    start(dirs, (4,), "fine", 6, STAR)
    for c in range(3):
        for plane in (1, 2):
            sol_ref[c, plane - 1] += dirs[3, c, plane, own, :] + dirs[4, c, plane, own, :]
    arrive(dirs, (4,), "fine", 6, STAR)
    relax(4, from_r2, into_r2, steps[2])
    start(dirs, (5,), "fine", 7, STAR)
    for c in range(3):
        for plane in (1, 2):
            sol_ref[c, plane - 1] += dirs[5, c, plane, own, :]
    arrive(dirs, (5,), "fine", 7, STAR)
    relax(5, from_r2, into_result, None)

    for ref, lead, kind, round_id, way in started:

        @pl.when(exists(*DIRS[way]))
        def _(ref=ref, lead=lead, kind=kind, round_id=round_id, way=way):
            message(ref, lead, kind, round_id, way).wait_send()

    for step in range(1, n_gy):
        sum_message(step).wait_send()


def solution(mesh):
    n_gx = mesh.shape["gx"]
    n_gy = mesh.shape["gy"]

    def shards(rhs_field, shear_modulus, lame_lambda, group_start):
        _, planes, rows, lanes = rhs_field.shape
        assert planes == 2
        ext = rows + 2 * H
        vmem = pl.BlockSpec(memory_space=pltpu.VMEM)
        field = jax.ShapeDtypeStruct(rhs_field.shape, jnp.float32)
        f32 = jnp.float32
        return pl.pallas_call(
            functools.partial(kernel, n_gx, n_gy),
            out_shape=(field, field),
            in_specs=[vmem, vmem, vmem, pl.BlockSpec(memory_space=pltpu.SMEM)],
            out_specs=(vmem, vmem),
            scratch_shapes=[
                pltpu.VMEM((2, 6, ext, lanes), f32),
                pltpu.VMEM((3, 4, ext, lanes), f32),
                pltpu.VMEM((3, 4, ext, lanes), f32),
                pltpu.VMEM((6, 3, 4, ext, lanes), f32),
                pltpu.VMEM((3, 4, ext, lanes), f32),
                pltpu.VMEM((3, 4, ext, lanes), f32),
                pltpu.VMEM((3, 3, ext, lanes), f32),
                pltpu.VMEM((n_gy, 8, lanes), f32),
                pltpu.SemaphoreType.DMA((8, 8)),
                pltpu.SemaphoreType.DMA((8, 8)),
                pltpu.SemaphoreType.DMA((n_gy,)),
                pltpu.SemaphoreType.DMA((n_gy,)),
            ],
            compiler_params=pltpu.CompilerParams(
                collective_id=0, has_side_effects=True, vmem_limit_bytes=24 * 1024 * 1024
            ),
            cost_estimate=pl.CostEstimate(
                flops=10_000_000, bytes_accessed=400_000, transcendentals=0
            ),
        )(rhs_field, shear_modulus, lame_lambda, group_start)

    return jax.shard_map(
        shards,
        mesh=mesh,
        in_specs=(
            P(None, "gx", "gy", None),
            P("gx", "gy", None),
            P("gx", "gy", None),
            P("gx", None),
        ),
        out_specs=(P(None, "gx", "gy", None), P(None, "gx", "gy", None)),
        check_vma=False,
    )
```

```python
import functools

import jax
import jax.numpy as jnp
from jax import lax
from jax.experimental import pallas as pl
from jax.experimental.pallas import tpu as pltpu
from jax.sharding import PartitionSpec as P

SWEEPS = 3
COARSE_SWEEPS = 4
LOW_BOUND = 0.5
HIGH_BOUND = 6.0
SHIFT_SCALE = 48.0

MID = 0.5 * (HIGH_BOUND + LOW_BOUND)
HALF = 0.5 * (HIGH_BOUND - LOW_BOUND)
SIGMA = MID / HALF

H = 8
DIRS = ((1, 0), (-1, 0), (0, 1), (0, -1), (1, -1), (-1, 1), (1, 1), (-1, -1))


def weights(steps):
    out = [(0.0, 1.0 / MID)]
    old = 1.0 / SIGMA
    for _ in range(steps - 1):
        new = 1.0 / (2.0 * SIGMA - old)
        out.append((new * old, 2.0 * new / HALF))
        old = new
    return out


def kernel(
    n_gx, n_gy, rhs_in, mu_in, lam_in, starts_in, sol_ref, res_ref,
    coef, rhs, inv, dirs, rbuf, r2buf, fc, sums, starts_ref, send, recv, sum_send, sum_recv, load_sem,
):
    rows = rhs_in.shape[2]
    lanes = rhs_in.shape[3]
    ext = rows + 2 * H
    gx = lax.axis_index("gx")
    gy = lax.axis_index("gy")
    own = slice(H, H + rows)

    def exists(sx, sy):
        ok = None
        for pos, step, count in ((gx, sx, n_gx), (gy, sy, n_gy)):
            if step == 1:
                here = pos < count - 1
            elif step == -1:
                here = pos > 0
            else:
                continue
            ok = here if ok is None else jnp.logical_and(ok, here)
        return ok

    barrier = pltpu.get_barrier_semaphore()
    expected = jnp.int32(n_gy - 1)
    for sx, sy in DIRS:
        if sx == 0:
            continue

        @pl.when(exists(sx, sy))
        def _(sx=sx, sy=sy):
            pl.semaphore_signal(
                barrier, inc=1, device_id=(gx + sx, gy + sy), device_id_type=pl.DeviceIdType.MESH
            )

        expected = expected + exists(sx, sy).astype(jnp.int32)
    for step in range(1, n_gy):
        pl.semaphore_signal(
            barrier,
            inc=1,
            device_id=(gx, lax.rem(gy + step, n_gy)),
            device_id_type=pl.DeviceIdType.MESH,
        )
    loads = [
        pltpu.make_async_copy(source, target, load_sem.at[k])
        for k, (source, target) in enumerate(
            (
                (mu_in, coef.at[0, 2:4, own]),
                (lam_in, coef.at[1, 2:4, own]),
                (rhs_in, rhs.at[:, 1:3, own]),
                (starts_in, starts_ref),
            )
        )
    ]
    for copy in loads:
        copy.start()

    def clear(ref, index):
        ref[index] = jnp.zeros_like(ref[index])

    every = slice(None)
    for edge, planes2, planes1, planef in (
        (gx == 0, slice(0, 2), 0, 0),
        (gx == n_gx - 1, slice(4, 6), 3, 2),
    ):

        @pl.when(edge)
        def _(planes2=planes2, planes1=planes1, planef=planef):
            clear(coef, (every, planes2))
            clear(rhs, (every, planes1))
            clear(rbuf, (every, planes1))
            clear(fc, (every, planef))
            for k in (1, 2, 4, 5):
                clear(dirs, (k, every, planes1))

    for edge, edge_rows in ((gy == 0, slice(0, H)), (gy == n_gy - 1, slice(H + rows, ext))):

        @pl.when(edge)
        def _(edge_rows=edge_rows):
            for ref in (coef, rhs, rbuf, fc):
                clear(ref, (every, every, edge_rows))
            for k in (1, 2, 4, 5):
                clear(dirs, (k, every, every, edge_rows))

    for copy in loads:
        copy.wait()
    pl.semaphore_wait(barrier, expected)

    def message(ref, lead, kind, round_id, way):
        sx, sy = DIRS[way]
        if kind == "coef":
            src_p = slice(2, 4)
            dst_p = {0: slice(2, 4), 1: slice(0, 2), -1: slice(4, 6)}[sx]
        elif kind == "fine":
            src_p = {0: slice(1, 3), 1: slice(2, 3), -1: slice(1, 2)}[sx]
            dst_p = {0: slice(1, 3), 1: slice(0, 1), -1: slice(3, 4)}[sx]
        else:
            src_p = slice(1, 2)
            dst_p = {0: slice(1, 2), 1: slice(0, 1), -1: slice(2, 3)}[sx]
        src_r = {0: own, 1: slice(rows, rows + H), -1: slice(H, 2 * H)}[sy]
        dst_r = {0: own, 1: slice(0, H), -1: slice(H + rows, ext)}[sy]
        return pltpu.make_async_remote_copy(
            src_ref=ref.at[lead + (every, src_p, src_r)],
            dst_ref=ref.at[lead + (every, dst_p, dst_r)],
            send_sem=send.at[round_id, way],
            recv_sem=recv.at[round_id, way],
            device_id=(gx + sx, gy + sy),
            device_id_type=pl.DeviceIdType.MESH,
        )

    started = []

    def start(ref, lead, kind, round_id, ways):
        for way in ways:
            started.append((ref, lead, kind, round_id, way))

            @pl.when(exists(*DIRS[way]))
            def _(way=way):
                message(ref, lead, kind, round_id, way).start()

    def arrive(ref, lead, kind, round_id, ways):
        for way in ways:
            sx, sy = DIRS[way]

            @pl.when(exists(-sx, -sy))
            def _(way=way):
                message(ref, lead, kind, round_id, way).wait_recv()

    ALL = range(8)
    STAR = range(6)
    start(coef, (), "coef", 0, ALL)
    start(rhs, (), "fine", 1, ALL)

    def lane_of(count):
        return lax.broadcasted_iota(jnp.int32, (count, lanes), 1)

    def make_zshift(count, dist):
        lane = lane_of(count)

        def up(a):
            return jnp.where(lane >= lanes - dist, 0.0, pltpu.roll(a, lanes - dist, 1))

        def down(a):
            return jnp.where(lane < dist, 0.0, pltpu.roll(a, dist, 1))

        return up, down

    def coef_at(which, plane, first, count):
        return coef[which, plane, first : first + count, :]

    def operate(load, plane, first, count):
        up, down = make_zshift(count, 1)

        def mu(dp, dy):
            return coef_at(0, plane + 1 + dp, first + dy, count)

        def lam(dp, dy):
            return coef_at(1, plane + 1 + dp, first + dy, count)

        m0 = mu(0, 0)
        faces = [
            0.5 * (m0 + mu(1, 0)),
            0.5 * (m0 + mu(-1, 0)),
            0.5 * (m0 + mu(0, 1)),
            0.5 * (m0 + mu(0, -1)),
            0.5 * (m0 + up(m0)),
            0.5 * (m0 + down(m0)),
        ]
        centre = [load(c, plane, 0, 0) for c in range(3)]
        vx_up = load(0, plane, 1, 0)
        vy_up = load(1, plane, 0, 1)
        vz_up = up(centre[2])
        here = lam(0, 0) * (
            (vx_up - centre[0]) + (vy_up - centre[1]) + (vz_up - centre[2])
        )
        vx_low = load(0, plane, -1, 0)
        vy_side = load(1, plane, -1, 0)
        vz_side = load(2, plane, -1, 0)
        back_x = lam(-1, 0) * (
            (centre[0] - vx_low)
            + (load(1, plane, -1, 1) - vy_side)
            + (up(vz_side) - vz_side)
        )
        vx_below = load(0, plane, 0, -1)
        vy_low = load(1, plane, 0, -1)
        vz_below = load(2, plane, 0, -1)
        back_y = lam(0, -1) * (
            (load(0, plane, 1, -1) - vx_below)
            + (centre[1] - vy_low)
            + (up(vz_below) - vz_below)
        )
        backs = [back_x, back_y, down(here)]
        out = []
        for c in range(3):
            v = centre[c]
            laplace = (
                faces[0] * ((vx_up if c == 0 else load(c, plane, 1, 0)) - v)
                - faces[1] * (v - load(c, plane, -1, 0))
                + faces[2] * ((vy_up if c == 1 else load(c, plane, 0, 1)) - v)
                - faces[3] * (v - load(c, plane, 0, -1))
                + faces[4] * ((vz_up if c == 2 else up(v)) - v)
                - faces[5] * (v - down(v))
            )
            out.append(-laplace - (here - backs[c]))
        return out

    def direction_load(k, first, count):
        def load(c, plane, dp, dy):
            return dirs[k, c, plane + dp, first + dy : first + dy + count, :]

        return load

    steps = weights(SWEEPS)

    arrive(coef, (), "coef", 0, ALL)
    wide_first, wide = H - 1, rows + 2
    up, down = make_zshift(wide, 1)
    row_id = lax.broadcasted_iota(jnp.int32, (wide, lanes), 0)
    row_ok = jnp.logical_and(
        jnp.logical_or(row_id > 0, gy > 0), jnp.logical_or(row_id < wide - 1, gy < n_gy - 1)
    )
    for plane in range(4):
        m0 = coef_at(0, plane + 1, wide_first, wide)
        l0 = coef_at(1, plane + 1, wide_first, wide)
        total = (
            0.5 * (m0 + coef_at(0, plane + 2, wide_first, wide))
            + 0.5 * (m0 + coef_at(0, plane, wide_first, wide))
            + 0.5 * (m0 + coef_at(0, plane + 1, wide_first + 1, wide))
            + 0.5 * (m0 + coef_at(0, plane + 1, wide_first - 1, wide))
            + 0.5 * (m0 + up(m0))
            + 0.5 * (m0 + down(m0))
            + l0
        )
        sides = (
            coef_at(1, plane, wide_first, wide),
            coef_at(1, plane + 1, wide_first - 1, wide),
            down(l0),
        )
        ok = row_ok
        if plane == 0:
            ok = jnp.logical_and(ok, gx > 0)
        if plane == 3:
            ok = jnp.logical_and(ok, gx < n_gx - 1)
        for c in range(3):
            inv[c, plane, wide_first : wide_first + wide, :] = jnp.where(
                ok, 1.0 / (total + sides[c]), 0.0
            )
    arrive(rhs, (), "fine", 1, ALL)
    wide_rows = slice(wide_first, wide_first + wide)
    for plane in range(4):
        for c in range(3):
            dirs[0, c, plane, wide_rows, :] = (
                steps[0][1] * inv[c, plane, wide_rows, :] * rhs[c, plane, wide_rows, :]
            )

    def relax(k, source, target, following):
        for plane in (1, 2):
            applied = operate(direction_load(k, H, rows), plane, H, rows)
            for c in range(3):
                left = source(c, plane) - applied[c]
                target(c, plane, left)
                if following is not None:
                    dirs[k + 1, c, plane, own, :] = (
                        following[0] * dirs[k, c, plane, own, :]
                        + following[1] * (inv[c, plane, own, :] * left)
                    )

    def into_rbuf(c, plane, value):
        rbuf[c, plane, own, :] = value

    def from_rbuf(c, plane):
        return rbuf[c, plane, own, :]

    relax(0, lambda c, plane: rhs[c, plane, own, :], into_rbuf, steps[1])
    start(dirs, (1,), "fine", 2, STAR)

    lane = lane_of(ext)
    rid = lax.broadcasted_iota(jnp.int32, (ext, lanes), 0)
    lane_even = lane % 2 == 0
    row_even = rid % 2 == 0

    def cube_sum(a):
        a = a + jnp.where(lane_even, pltpu.roll(a, lanes - 1, 1), pltpu.roll(a, 1, 1))
        return a + jnp.where(row_even, pltpu.roll(a, ext - 1, 0), pltpu.roll(a, 1, 0))

    labels = []
    label = jnp.int32(0)
    for j in range(n_gy):
        if j > 0:
            label = label + starts_ref[0, j]
        labels.append(label)
    mine = labels[0]
    before = labels[0] - 1
    after = labels[0] - 1
    for j in range(n_gy):
        mine = jnp.where(gy == j, labels[j], mine)
        if j > 0:
            before = jnp.where(gy == j, labels[j - 1], before)
        if j < n_gy - 1:
            after = jnp.where(gy == j, labels[j + 1], after)
    low_open = jnp.logical_and(gy > 0, before == mine)
    high_open = jnp.logical_and(gy < n_gy - 1, after == mine)
    inside = jnp.logical_and(
        jnp.logical_or(rid >= H, low_open), jnp.logical_or(rid < H + rows, high_open)
    )
    up2, down2 = make_zshift(ext, 2)

    def row_up(a):
        return pltpu.roll(a, ext - 2, 0)

    def row_down(a):
        return pltpu.roll(a, 2, 0)

    cmu = jnp.where(inside, 0.125 * cube_sum(coef[0, 2] + coef[0, 3]), 0.0)
    clam = jnp.where(inside, 0.125 * cube_sum(coef[1, 2] + coef[1, 3]), 0.0)
    cf = [
        0.5 * (cmu + row_up(cmu)),
        0.5 * (cmu + row_down(cmu)),
        0.5 * (cmu + up2(cmu)),
        0.5 * (cmu + down2(cmu)),
    ]
    csum = cmu + cf[0] + cf[1] + cf[2] + cf[3]
    cinv = [
        jnp.where(inside, 1.0 / (4.0 * (csum + clam + side)), 0.0)
        for side in (0.0, row_down(clam), down2(clam))
    ]

    def coarse_operate(v):
        vy_up = row_up(v[1])
        vz_up = up2(v[2])
        here = clam * ((vy_up - v[1]) + (vz_up - v[2]) - v[0])
        backs = [0.0, row_down(here), down2(here)]
        out = []
        for c in range(3):
            laplace = (
                cf[0] * ((vy_up if c == 1 else row_up(v[c])) - v[c])
                - cf[1] * (v[c] - row_down(v[c]))
                + cf[2] * ((vz_up if c == 2 else up2(v[c])) - v[c])
                - cf[3] * (v[c] - down2(v[c]))
                - cmu * v[c]
            )
            out.append(4.0 * (-laplace - (here - backs[c])))
        return out

    for c in range(3):
        for plane in (1, 2):
            sol_ref[c, plane - 1] = dirs[0, c, plane, own, :] + dirs[1, c, plane, own, :]
    arrive(dirs, (1,), "fine", 2, STAR)
    relax(1, from_rbuf, into_rbuf, steps[2])
    start(dirs, (2,), "fine", 3, STAR)
    for c in range(3):
        for plane in (1, 2):
            sol_ref[c, plane - 1] += dirs[2, c, plane, own, :]
    arrive(dirs, (2,), "fine", 3, STAR)
    relax(2, from_rbuf, into_rbuf, None)
    start(rbuf, (), "fine", 4, (2, 3, 0, 1, 4, 5, 6, 7))

    sub = lax.broadcasted_iota(jnp.int32, (8, lanes), 0)
    part = jnp.zeros((8, lanes), jnp.float32)
    for c in range(3):
        both = rbuf[c, 1, own, :] + rbuf[c, 2, own, :]
        part = jnp.where(sub == c, jnp.sum(both, axis=0, keepdims=True), part)
    sums[0] = part

    def sum_message(step):
        return pltpu.make_async_remote_copy(
            src_ref=sums.at[0],
            dst_ref=sums.at[step],
            send_sem=sum_send.at[step],
            recv_sem=sum_recv.at[step],
            device_id=(gx, lax.rem(gy + step, n_gy)),
            device_id_type=pl.DeviceIdType.MESH,
        )

    for step in range(1, n_gy):
        sum_message(step).start()

    arrive(rbuf, (), "fine", 4, (2, 3))
    left = [
        jnp.where(inside, cube_sum(rbuf[c, 1] + rbuf[c, 2]), 0.0) for c in range(3)
    ]
    coarse_steps = weights(COARSE_SWEEPS)
    direction = [coarse_steps[0][1] * cinv[c] * left[c] for c in range(3)]
    smoothed = direction
    for old, new in coarse_steps[1:]:
        applied = coarse_operate(direction)
        left = [left[c] - applied[c] for c in range(3)]
        direction = [old * direction[c] + new * (cinv[c] * left[c]) for c in range(3)]
        smoothed = [smoothed[c] + direction[c] for c in range(3)]

    total = sums[0]
    members = jnp.float32(1.0)
    for step in range(1, n_gy):
        sum_message(step).wait_recv()
        source = lax.rem(gy + n_gy - step, n_gy)
        other = labels[0]
        for j in range(1, n_gy):
            other = jnp.where(source == j, labels[j], other)
        same = jnp.where(other == mine, jnp.float32(1.0), jnp.float32(0.0))
        total = total + same * sums[step]
        members = members + same
    cells_dev = (rows // 2) * (lanes // 2)
    scale = jnp.full((8, 1), SHIFT_SCALE * cells_dev, jnp.float32) * members
    shift = jnp.sum(total, axis=1, keepdims=True) / scale
    for c in range(3):
        fc[c, 1, own, :] = smoothed[c][H : H + rows] + shift[c : c + 1, :]
    start(fc, (), "coarse", 5, ALL)
    for c in range(3):
        for plane in (1, 2):
            sol_ref[c, plane - 1] += fc[c, 1, own, :]
    arrive(rbuf, (), "fine", 4, (0, 1, 4, 5, 6, 7))
    arrive(fc, (), "coarse", 5, ALL)

    def fc_load(c, plane, dp, dy):
        return fc[c, (plane + 1 + dp) // 2, wide_first + dy : wide_first + dy + wide, :]

    for plane in range(4):
        applied = operate(fc_load, plane, wide_first, wide)
        for c in range(3):
            value = rbuf[c, plane, wide_rows, :] - applied[c]
            r2buf[c, plane, wide_rows, :] = value
            dirs[3, c, plane, wide_rows, :] = steps[0][1] * inv[c, plane, wide_rows, :] * value

    def into_r2(c, plane, value):
        r2buf[c, plane, own, :] = value

    def from_r2(c, plane):
        return r2buf[c, plane, own, :]

    def into_result(c, plane, value):
        res_ref[c, plane - 1] = value

    relax(3, from_r2, into_r2, steps[1])
    start(dirs, (4,), "fine", 6, STAR)
    for c in range(3):
        for plane in (1, 2):
            sol_ref[c, plane - 1] += dirs[3, c, plane, own, :] + dirs[4, c, plane, own, :]
    arrive(dirs, (4,), "fine", 6, STAR)
    relax(4, from_r2, into_r2, steps[2])
    start(dirs, (5,), "fine", 7, STAR)
    for c in range(3):
        for plane in (1, 2):
            sol_ref[c, plane - 1] += dirs[5, c, plane, own, :]
    arrive(dirs, (5,), "fine", 7, STAR)
    relax(5, from_r2, into_result, None)

    for ref, lead, kind, round_id, way in started:

        @pl.when(exists(*DIRS[way]))
        def _(ref=ref, lead=lead, kind=kind, round_id=round_id, way=way):
            message(ref, lead, kind, round_id, way).wait_send()

    for step in range(1, n_gy):
        sum_message(step).wait_send()


def solution(mesh):
    n_gx = mesh.shape["gx"]
    n_gy = mesh.shape["gy"]

    def shards(rhs_field, shear_modulus, lame_lambda, group_start):
        _, planes, rows, lanes = rhs_field.shape
        assert planes == 2
        ext = rows + 2 * H
        vmem = pl.BlockSpec(memory_space=pltpu.VMEM)
        hbm = pl.BlockSpec(memory_space=pltpu.MemorySpace.HBM)
        field = jax.ShapeDtypeStruct(rhs_field.shape, jnp.float32)
        f32 = jnp.float32
        return pl.pallas_call(
            functools.partial(kernel, n_gx, n_gy),
            out_shape=(field, field),
            in_specs=[hbm, hbm, hbm, hbm],
            out_specs=(vmem, vmem),
            scratch_shapes=[
                pltpu.VMEM((2, 6, ext, lanes), f32),
                pltpu.VMEM((3, 4, ext, lanes), f32),
                pltpu.VMEM((3, 4, ext, lanes), f32),
                pltpu.VMEM((6, 3, 4, ext, lanes), f32),
                pltpu.VMEM((3, 4, ext, lanes), f32),
                pltpu.VMEM((3, 4, ext, lanes), f32),
                pltpu.VMEM((3, 3, ext, lanes), f32),
                pltpu.VMEM((n_gy, 8, lanes), f32),
                pltpu.SMEM((1, n_gy), jnp.int32),
                pltpu.SemaphoreType.DMA((8, 8)),
                pltpu.SemaphoreType.DMA((8, 8)),
                pltpu.SemaphoreType.DMA((n_gy,)),
                pltpu.SemaphoreType.DMA((n_gy,)),
                pltpu.SemaphoreType.DMA((4,)),
            ],
            compiler_params=pltpu.CompilerParams(
                collective_id=0, has_side_effects=True, vmem_limit_bytes=24 * 1024 * 1024
            ),
            cost_estimate=pl.CostEstimate(
                flops=10_000_000, bytes_accessed=400_000, transcendentals=0
            ),
        )(rhs_field, shear_modulus, lame_lambda, group_start)

    return jax.shard_map(
        shards,
        mesh=mesh,
        in_specs=(
            P(None, "gx", "gy", None),
            P("gx", "gy", None),
            P("gx", "gy", None),
            P("gx", None),
        ),
        out_specs=(P(None, "gx", "gy", None), P(None, "gx", "gy", None)),
        check_vma=False,
    )
```

```python
import functools

import jax
import jax.numpy as jnp
from jax import lax
from jax.experimental import pallas as pl
from jax.experimental.pallas import tpu as pltpu
from jax.sharding import PartitionSpec as P

SWEEPS = 3
COARSE_SWEEPS = 4
LOW_BOUND = 0.5
HIGH_BOUND = 6.0
SHIFT_SCALE = 48.0

MID = 0.5 * (HIGH_BOUND + LOW_BOUND)
HALF = 0.5 * (HIGH_BOUND - LOW_BOUND)
SIGMA = MID / HALF

H = 8
DIRS = ((1, 0), (-1, 0), (0, 1), (0, -1), (1, -1), (-1, 1), (1, 1), (-1, -1),
        (2, 0), (-2, 0), (2, -1), (-2, 1))


def weights(steps):
    out = [(0.0, 1.0 / MID)]
    old = 1.0 / SIGMA
    for _ in range(steps - 1):
        new = 1.0 / (2.0 * SIGMA - old)
        out.append((new * old, 2.0 * new / HALF))
        old = new
    return out


def kernel(
    n_gx, n_gy, rhs_in, mu_in, lam_in, starts_in, sol_ref, res_ref,
    coef, rhs, inv, dirs, rbuf, r2buf, fc, sums, starts_ref, send, recv, sum_send, sum_recv, load_sem,
):
    rows = rhs_in.shape[2]
    lanes = rhs_in.shape[3]
    ext = rows + 2 * H
    gx = lax.axis_index("gx")
    gy = lax.axis_index("gy")
    own = slice(H, H + rows)

    def exists(sx, sy):
        ok = None
        for pos, step, count in ((gx, sx, n_gx), (gy, sy, n_gy)):
            if step == 0:
                continue
            here = pos < count - step if step > 0 else pos >= -step
            ok = here if ok is None else jnp.logical_and(ok, here)
        return ok

    barrier = pltpu.get_barrier_semaphore()
    expected = jnp.int32(n_gy - 1)
    for sx, sy in DIRS:
        if sx == 0:
            continue

        @pl.when(exists(sx, sy))
        def _(sx=sx, sy=sy):
            pl.semaphore_signal(
                barrier, inc=1, device_id=(gx + sx, gy + sy), device_id_type=pl.DeviceIdType.MESH
            )

        expected = expected + exists(sx, sy).astype(jnp.int32)
    for step in range(1, n_gy):
        pl.semaphore_signal(
            barrier,
            inc=1,
            device_id=(gx, lax.rem(gy + step, n_gy)),
            device_id_type=pl.DeviceIdType.MESH,
        )
    loads = [
        pltpu.make_async_copy(source, target, load_sem.at[k])
        for k, (source, target) in enumerate(
            (
                (mu_in, coef.at[0, 3:5, own]),
                (lam_in, coef.at[1, 3:5, own]),
                (rhs_in, rhs.at[:, 2:4, own]),
                (starts_in, starts_ref),
            )
        )
    ]
    for copy in loads:
        copy.start()

    def clear(ref, index):
        ref[index] = jnp.zeros_like(ref[index])

    every = slice(None)
    for edge, planes2, planes1, planef in (
        (gx == 0, slice(0, 3), slice(0, 2), slice(0, 2)),
        (gx == n_gx - 1, slice(5, 8), slice(4, 6), slice(3, 5)),
    ):

        @pl.when(edge)
        def _(planes2=planes2, planes1=planes1, planef=planef):
            clear(coef, (every, planes2))
            clear(rhs, (every, planes1))
            clear(rbuf, (every, planes1))
            clear(fc, (every, planef))
            for k in (2, 5):
                clear(dirs, (k, every, planes1))

    for edge, plane_c, plane_f in ((gx == 1, 0, 0), (gx == n_gx - 2, 7, 4)):

        @pl.when(edge)
        def _(plane_c=plane_c, plane_f=plane_f):
            clear(coef, (every, plane_c))
            clear(fc, (every, plane_f))

    for edge, edge_rows in ((gy == 0, slice(0, H)), (gy == n_gy - 1, slice(H + rows, ext))):

        @pl.when(edge)
        def _(edge_rows=edge_rows):
            for ref in (coef, rhs, rbuf, fc):
                clear(ref, (every, every, edge_rows))
            for k in (2, 5):
                clear(dirs, (k, every, every, edge_rows))

    for copy in loads:
        copy.wait()
    pl.semaphore_wait(barrier, expected)

    def message(ref, lead, kind, round_id, way):
        sx, sy = DIRS[way]
        if kind == "coef":
            src_p = {2: slice(4, 5), -2: slice(3, 4)}.get(sx, slice(3, 5))
            dst_p = {
                0: slice(3, 5), 1: slice(1, 3), -1: slice(5, 7), 2: slice(0, 1), -2: slice(7, 8)
            }[sx]
        elif kind == "deep":
            src_p = slice(2, 4)
            dst_p = {0: slice(2, 4), 1: slice(0, 2), -1: slice(4, 6)}[sx]
        elif kind == "fine":
            src_p = {0: slice(2, 4), 1: slice(3, 4), -1: slice(2, 3)}[sx]
            dst_p = {0: slice(2, 4), 1: slice(1, 2), -1: slice(4, 5)}[sx]
        else:
            src_p = slice(2, 3)
            dst_p = {
                0: slice(2, 3), 1: slice(1, 2), -1: slice(3, 4), 2: slice(0, 1), -2: slice(4, 5)
            }[sx]
        src_r = {0: own, 1: slice(rows, rows + H), -1: slice(H, 2 * H)}[sy]
        dst_r = {0: own, 1: slice(0, H), -1: slice(H + rows, ext)}[sy]
        return pltpu.make_async_remote_copy(
            src_ref=ref.at[lead + (every, src_p, src_r)],
            dst_ref=ref.at[lead + (every, dst_p, dst_r)],
            send_sem=send.at[round_id, way],
            recv_sem=recv.at[round_id, way],
            device_id=(gx + sx, gy + sy),
            device_id_type=pl.DeviceIdType.MESH,
        )

    started = []

    def start(ref, lead, kind, round_id, ways):
        for way in ways:
            started.append((ref, lead, kind, round_id, way))

            @pl.when(exists(*DIRS[way]))
            def _(way=way):
                message(ref, lead, kind, round_id, way).start()

    def arrive(ref, lead, kind, round_id, ways):
        for way in ways:
            sx, sy = DIRS[way]

            @pl.when(exists(-sx, -sy))
            def _(way=way):
                message(ref, lead, kind, round_id, way).wait_recv()

    ALL = range(12)
    NEAR = range(8)
    STAR = range(6)
    start(coef, (), "coef", 0, ALL)
    start(rhs, (), "deep", 1, NEAR)

    def lane_of(count):
        return lax.broadcasted_iota(jnp.int32, (count, lanes), 1)

    def make_zshift(count, dist):
        lane = lane_of(count)

        def up(a):
            return jnp.where(lane >= lanes - dist, 0.0, pltpu.roll(a, lanes - dist, 1))

        def down(a):
            return jnp.where(lane < dist, 0.0, pltpu.roll(a, dist, 1))

        return up, down

    def coef_at(which, plane, first, count):
        return coef[which, plane, first : first + count, :]

    def operate(load, plane, first, count):
        up, down = make_zshift(count, 1)

        def mu(dp, dy):
            return coef_at(0, plane + 1 + dp, first + dy, count)

        def lam(dp, dy):
            return coef_at(1, plane + 1 + dp, first + dy, count)

        m0 = mu(0, 0)
        faces = [
            0.5 * (m0 + mu(1, 0)),
            0.5 * (m0 + mu(-1, 0)),
            0.5 * (m0 + mu(0, 1)),
            0.5 * (m0 + mu(0, -1)),
            0.5 * (m0 + up(m0)),
            0.5 * (m0 + down(m0)),
        ]
        centre = [load(c, plane, 0, 0) for c in range(3)]
        vx_up = load(0, plane, 1, 0)
        vy_up = load(1, plane, 0, 1)
        vz_up = up(centre[2])
        here = lam(0, 0) * (
            (vx_up - centre[0]) + (vy_up - centre[1]) + (vz_up - centre[2])
        )
        vx_low = load(0, plane, -1, 0)
        vy_side = load(1, plane, -1, 0)
        vz_side = load(2, plane, -1, 0)
        back_x = lam(-1, 0) * (
            (centre[0] - vx_low)
            + (load(1, plane, -1, 1) - vy_side)
            + (up(vz_side) - vz_side)
        )
        vx_below = load(0, plane, 0, -1)
        vy_low = load(1, plane, 0, -1)
        vz_below = load(2, plane, 0, -1)
        back_y = lam(0, -1) * (
            (load(0, plane, 1, -1) - vx_below)
            + (centre[1] - vy_low)
            + (up(vz_below) - vz_below)
        )
        backs = [back_x, back_y, down(here)]
        out = []
        for c in range(3):
            v = centre[c]
            laplace = (
                faces[0] * ((vx_up if c == 0 else load(c, plane, 1, 0)) - v)
                - faces[1] * (v - load(c, plane, -1, 0))
                + faces[2] * ((vy_up if c == 1 else load(c, plane, 0, 1)) - v)
                - faces[3] * (v - load(c, plane, 0, -1))
                + faces[4] * ((vz_up if c == 2 else up(v)) - v)
                - faces[5] * (v - down(v))
            )
            out.append(-laplace - (here - backs[c]))
        return out

    def direction_load(k, first, count):
        def load(c, plane, dp, dy):
            return dirs[k, c, plane + dp, first + dy : first + dy + count, :]

        return load

    steps = weights(SWEEPS)

    arrive(coef, (), "coef", 0, ALL)
    wide_first, wide = H - 2, rows + 4
    up, down = make_zshift(wide, 1)
    row_id = lax.broadcasted_iota(jnp.int32, (wide, lanes), 0)
    row_ok = jnp.logical_and(
        jnp.logical_or(row_id > 1, gy > 0), jnp.logical_or(row_id < wide - 2, gy < n_gy - 1)
    )
    for plane in range(6):
        m0 = coef_at(0, plane + 1, wide_first, wide)
        l0 = coef_at(1, plane + 1, wide_first, wide)
        total = (
            0.5 * (m0 + coef_at(0, plane + 2, wide_first, wide))
            + 0.5 * (m0 + coef_at(0, plane, wide_first, wide))
            + 0.5 * (m0 + coef_at(0, plane + 1, wide_first + 1, wide))
            + 0.5 * (m0 + coef_at(0, plane + 1, wide_first - 1, wide))
            + 0.5 * (m0 + up(m0))
            + 0.5 * (m0 + down(m0))
            + l0
        )
        sides = (
            coef_at(1, plane, wide_first, wide),
            coef_at(1, plane + 1, wide_first - 1, wide),
            down(l0),
        )
        ok = row_ok
        if plane < 2:
            ok = jnp.logical_and(ok, gx > 0)
        if plane > 3:
            ok = jnp.logical_and(ok, gx < n_gx - 1)
        for c in range(3):
            inv[c, plane, wide_first : wide_first + wide, :] = jnp.where(
                ok, 1.0 / (total + sides[c]), 0.0
            )
    arrive(rhs, (), "deep", 1, NEAR)
    wide_rows = slice(wide_first, wide_first + wide)
    for plane in range(6):
        for c in range(3):
            dirs[0, c, plane, wide_rows, :] = (
                steps[0][1] * inv[c, plane, wide_rows, :] * rhs[c, plane, wide_rows, :]
            )

    def relax(k, source, target, following, planes, first, count):
        some = slice(first, first + count)
        for plane in planes:
            applied = operate(direction_load(k, first, count), plane, first, count)
            for c in range(3):
                left = source[c, plane, some, :] - applied[c]
                if target is None:
                    res_ref[c, plane - 2] = left
                else:
                    target[c, plane, some, :] = left
                if following is not None:
                    dirs[k + 1, c, plane, some, :] = (
                        following[0] * dirs[k, c, plane, some, :]
                        + following[1] * (inv[c, plane, some, :] * left)
                    )

    BEYOND = ((1, 2, 3, 4), H - 1, rows + 2)
    BLOCK = ((2, 3), H, rows)
    relax(0, rhs, r2buf, steps[1], *BEYOND)
    relax(1, r2buf, r2buf, steps[2], *BLOCK)
    start(dirs, (2,), "fine", 2, STAR)

    lane = lane_of(ext)
    rid = lax.broadcasted_iota(jnp.int32, (ext, lanes), 0)
    lane_even = lane % 2 == 0
    row_even = rid % 2 == 0

    def cube_sum(a):
        a = a + jnp.where(lane_even, pltpu.roll(a, lanes - 1, 1), pltpu.roll(a, 1, 1))
        return a + jnp.where(row_even, pltpu.roll(a, ext - 1, 0), pltpu.roll(a, 1, 0))

    labels = []
    label = jnp.int32(0)
    for j in range(n_gy):
        if j > 0:
            label = label + starts_ref[0, j]
        labels.append(label)
    mine = labels[0]
    before = labels[0] - 1
    after = labels[0] - 1
    for j in range(n_gy):
        mine = jnp.where(gy == j, labels[j], mine)
        if j > 0:
            before = jnp.where(gy == j, labels[j - 1], before)
        if j < n_gy - 1:
            after = jnp.where(gy == j, labels[j + 1], after)
    low_open = jnp.logical_and(gy > 0, before == mine)
    high_open = jnp.logical_and(gy < n_gy - 1, after == mine)
    inside = jnp.logical_and(
        jnp.logical_or(rid >= H, low_open), jnp.logical_or(rid < H + rows, high_open)
    )
    up2, down2 = make_zshift(ext, 2)

    def row_up(a):
        return pltpu.roll(a, ext - 2, 0)

    def row_down(a):
        return pltpu.roll(a, 2, 0)

    cmu = jnp.where(inside, 0.125 * cube_sum(coef[0, 3] + coef[0, 4]), 0.0)
    clam = jnp.where(inside, 0.125 * cube_sum(coef[1, 3] + coef[1, 4]), 0.0)
    cf = [
        0.5 * (cmu + row_up(cmu)),
        0.5 * (cmu + row_down(cmu)),
        0.5 * (cmu + up2(cmu)),
        0.5 * (cmu + down2(cmu)),
    ]
    csum = cmu + cf[0] + cf[1] + cf[2] + cf[3]
    cinv = [
        jnp.where(inside, 1.0 / (4.0 * (csum + clam + side)), 0.0)
        for side in (0.0, row_down(clam), down2(clam))
    ]

    def coarse_operate(v):
        vy_up = row_up(v[1])
        vz_up = up2(v[2])
        here = clam * ((vy_up - v[1]) + (vz_up - v[2]) - v[0])
        backs = [0.0, row_down(here), down2(here)]
        out = []
        for c in range(3):
            laplace = (
                cf[0] * ((vy_up if c == 1 else row_up(v[c])) - v[c])
                - cf[1] * (v[c] - row_down(v[c]))
                + cf[2] * ((vz_up if c == 2 else up2(v[c])) - v[c])
                - cf[3] * (v[c] - down2(v[c]))
                - cmu * v[c]
            )
            out.append(4.0 * (-laplace - (here - backs[c])))
        return out

    for c in range(3):
        for plane in (2, 3):
            sol_ref[c, plane - 2] = (
                dirs[0, c, plane, own, :]
                + dirs[1, c, plane, own, :]
                + dirs[2, c, plane, own, :]
            )
    arrive(dirs, (2,), "fine", 2, STAR)
    relax(2, r2buf, rbuf, None, *BLOCK)
    start(rbuf, (), "deep", 3, (2, 3, 0, 1, 4, 5, 6, 7))

    sub = lax.broadcasted_iota(jnp.int32, (8, lanes), 0)
    part = jnp.zeros((8, lanes), jnp.float32)
    for c in range(3):
        both = rbuf[c, 2, own, :] + rbuf[c, 3, own, :]
        part = jnp.where(sub == c, jnp.sum(both, axis=0, keepdims=True), part)
    sums[0] = part

    def sum_message(step):
        return pltpu.make_async_remote_copy(
            src_ref=sums.at[0],
            dst_ref=sums.at[step],
            send_sem=sum_send.at[step],
            recv_sem=sum_recv.at[step],
            device_id=(gx, lax.rem(gy + step, n_gy)),
            device_id_type=pl.DeviceIdType.MESH,
        )

    for step in range(1, n_gy):
        sum_message(step).start()

    arrive(rbuf, (), "deep", 3, (2, 3))
    left = [
        jnp.where(inside, cube_sum(rbuf[c, 2] + rbuf[c, 3]), 0.0) for c in range(3)
    ]
    coarse_steps = weights(COARSE_SWEEPS)
    direction = [coarse_steps[0][1] * cinv[c] * left[c] for c in range(3)]
    smoothed = direction
    for old, new in coarse_steps[1:]:
        applied = coarse_operate(direction)
        left = [left[c] - applied[c] for c in range(3)]
        direction = [old * direction[c] + new * (cinv[c] * left[c]) for c in range(3)]
        smoothed = [smoothed[c] + direction[c] for c in range(3)]

    total = sums[0]
    members = jnp.float32(1.0)
    for step in range(1, n_gy):
        sum_message(step).wait_recv()
        source = lax.rem(gy + n_gy - step, n_gy)
        other = labels[0]
        for j in range(1, n_gy):
            other = jnp.where(source == j, labels[j], other)
        same = jnp.where(other == mine, jnp.float32(1.0), jnp.float32(0.0))
        total = total + same * sums[step]
        members = members + same
    cells_dev = (rows // 2) * (lanes // 2)
    scale = jnp.full((8, 1), SHIFT_SCALE * cells_dev, jnp.float32) * members
    shift = jnp.sum(total, axis=1, keepdims=True) / scale
    for c in range(3):
        fc[c, 2, own, :] = smoothed[c][H : H + rows] + shift[c : c + 1, :]
    start(fc, (), "coarse", 4, ALL)
    for c in range(3):
        for plane in (2, 3):
            sol_ref[c, plane - 2] += fc[c, 2, own, :]
    arrive(rbuf, (), "deep", 3, (0, 1, 4, 5, 6, 7))
    arrive(fc, (), "coarse", 4, ALL)

    def fc_load(c, plane, dp, dy):
        return fc[c, (plane + 2 + dp) // 2, wide_first + dy : wide_first + dy + wide, :]

    for plane in range(6):
        applied = operate(fc_load, plane, wide_first, wide)
        for c in range(3):
            value = rbuf[c, plane, wide_rows, :] - applied[c]
            r2buf[c, plane, wide_rows, :] = value
            dirs[3, c, plane, wide_rows, :] = steps[0][1] * inv[c, plane, wide_rows, :] * value

    relax(3, r2buf, r2buf, steps[1], *BEYOND)
    relax(4, r2buf, r2buf, steps[2], *BLOCK)
    start(dirs, (5,), "fine", 5, STAR)
    for c in range(3):
        for plane in (2, 3):
            sol_ref[c, plane - 2] += (
                dirs[3, c, plane, own, :]
                + dirs[4, c, plane, own, :]
                + dirs[5, c, plane, own, :]
            )
    arrive(dirs, (5,), "fine", 5, STAR)
    relax(5, r2buf, None, None, *BLOCK)

    for ref, lead, kind, round_id, way in started:

        @pl.when(exists(*DIRS[way]))
        def _(ref=ref, lead=lead, kind=kind, round_id=round_id, way=way):
            message(ref, lead, kind, round_id, way).wait_send()

    for step in range(1, n_gy):
        sum_message(step).wait_send()


def solution(mesh):
    n_gx = mesh.shape["gx"]
    n_gy = mesh.shape["gy"]

    def shards(rhs_field, shear_modulus, lame_lambda, group_start):
        _, planes, rows, lanes = rhs_field.shape
        assert planes == 2
        ext = rows + 2 * H
        vmem = pl.BlockSpec(memory_space=pltpu.VMEM)
        hbm = pl.BlockSpec(memory_space=pltpu.MemorySpace.HBM)
        field = jax.ShapeDtypeStruct(rhs_field.shape, jnp.float32)
        f32 = jnp.float32
        return pl.pallas_call(
            functools.partial(kernel, n_gx, n_gy),
            out_shape=(field, field),
            in_specs=[hbm, hbm, hbm, hbm],
            out_specs=(vmem, vmem),
            scratch_shapes=[
                pltpu.VMEM((2, 8, ext, lanes), f32),
                pltpu.VMEM((3, 6, ext, lanes), f32),
                pltpu.VMEM((3, 6, ext, lanes), f32),
                pltpu.VMEM((6, 3, 6, ext, lanes), f32),
                pltpu.VMEM((3, 6, ext, lanes), f32),
                pltpu.VMEM((3, 6, ext, lanes), f32),
                pltpu.VMEM((3, 5, ext, lanes), f32),
                pltpu.VMEM((n_gy, 8, lanes), f32),
                pltpu.SMEM((1, n_gy), jnp.int32),
                pltpu.SemaphoreType.DMA((6, 12)),
                pltpu.SemaphoreType.DMA((6, 12)),
                pltpu.SemaphoreType.DMA((n_gy,)),
                pltpu.SemaphoreType.DMA((n_gy,)),
                pltpu.SemaphoreType.DMA((4,)),
            ],
            compiler_params=pltpu.CompilerParams(
                collective_id=0, has_side_effects=True
            ),
            cost_estimate=pl.CostEstimate(
                flops=10_000_000, bytes_accessed=400_000, transcendentals=0
            ),
        )(rhs_field, shear_modulus, lame_lambda, group_start)

    return jax.shard_map(
        shards,
        mesh=mesh,
        in_specs=(
            P(None, "gx", "gy", None),
            P("gx", "gy", None),
            P("gx", "gy", None),
            P("gx", None),
        ),
        out_specs=(P(None, "gx", "gy", None), P(None, "gx", "gy", None)),
        check_vma=False,
    )
```

```python
import functools

import jax
import jax.numpy as jnp
from jax import lax
from jax.experimental import pallas as pl
from jax.experimental.pallas import tpu as pltpu
from jax.sharding import PartitionSpec as P

SWEEPS = 3
COARSE_SWEEPS = 4
LOW_BOUND = 0.5
HIGH_BOUND = 6.0
SHIFT_SCALE = 48.0

MID = 0.5 * (HIGH_BOUND + LOW_BOUND)
HALF = 0.5 * (HIGH_BOUND - LOW_BOUND)
SIGMA = MID / HALF

H = 8
DIRS = ((1, 0), (-1, 0), (0, 1), (0, -1), (1, -1), (-1, 1), (1, 1), (-1, -1))


def weights(steps):
    out = [(0.0, 1.0 / MID)]
    old = 1.0 / SIGMA
    for _ in range(steps - 1):
        new = 1.0 / (2.0 * SIGMA - old)
        out.append((new * old, 2.0 * new / HALF))
        old = new
    return out


def kernel(
    n_gx, n_gy, rhs_in, mu_in, lam_in, starts_in, sol_ref, res_ref,
    coef, rhs, inv, dirs, rbuf, r2buf, fc, sums, starts_ref, send, recv, sum_send, sum_recv, load_sem,
):
    rows = rhs_in.shape[2]
    lanes = rhs_in.shape[3]
    ext = rows + 2 * H
    gx = lax.axis_index("gx")
    gy = lax.axis_index("gy")
    own = slice(H, H + rows)

    def exists(sx, sy):
        ok = None
        for pos, step, count in ((gx, sx, n_gx), (gy, sy, n_gy)):
            if step == 1:
                here = pos < count - 1
            elif step == -1:
                here = pos > 0
            else:
                continue
            ok = here if ok is None else jnp.logical_and(ok, here)
        return ok

    barrier = pltpu.get_barrier_semaphore()
    expected = jnp.int32(n_gy - 1)
    for sx, sy in DIRS:
        if sx == 0:
            continue

        @pl.when(exists(sx, sy))
        def _(sx=sx, sy=sy):
            pl.semaphore_signal(
                barrier, inc=1, device_id=(gx + sx, gy + sy), device_id_type=pl.DeviceIdType.MESH
            )

        expected = expected + exists(sx, sy).astype(jnp.int32)
    for step in range(1, n_gy):
        pl.semaphore_signal(
            barrier,
            inc=1,
            device_id=(gx, lax.rem(gy + step, n_gy)),
            device_id_type=pl.DeviceIdType.MESH,
        )
    loads = [
        pltpu.make_async_copy(source, target, load_sem.at[k])
        for k, (source, target) in enumerate(
            (
                (mu_in, coef.at[0, 2:4, own]),
                (lam_in, coef.at[1, 2:4, own]),
                (rhs_in, rhs.at[:, 1:3, own]),
                (starts_in, starts_ref),
            )
        )
    ]
    for copy in loads:
        copy.start()

    def clear(ref, index):
        ref[index] = jnp.zeros_like(ref[index])

    every = slice(None)
    for edge, planes2, planes1, planef in (
        (gx == 0, slice(0, 2), 0, 0),
        (gx == n_gx - 1, slice(4, 6), 3, 2),
    ):

        @pl.when(edge)
        def _(planes2=planes2, planes1=planes1, planef=planef):
            clear(coef, (every, planes2))
            clear(rhs, (every, planes1))
            clear(rbuf, (every, planes1))
            clear(fc, (every, planef))
            for k in (1, 2, 4, 5):
                clear(dirs, (k, every, planes1))

    for edge, edge_rows in ((gy == 0, slice(0, H)), (gy == n_gy - 1, slice(H + rows, ext))):

        @pl.when(edge)
        def _(edge_rows=edge_rows):
            for ref in (coef, rhs, rbuf, fc):
                clear(ref, (every, every, edge_rows))
            for k in (1, 2, 4, 5):
                clear(dirs, (k, every, every, edge_rows))

    for copy in loads:
        copy.wait()
    pl.semaphore_wait(barrier, expected)

    def message(ref, lead, kind, round_id, way):
        sx, sy = DIRS[way]
        if kind == "coef":
            src_p = slice(2, 4)
            dst_p = {0: slice(2, 4), 1: slice(0, 2), -1: slice(4, 6)}[sx]
        elif kind == "fine":
            src_p = {0: slice(1, 3), 1: slice(2, 3), -1: slice(1, 2)}[sx]
            dst_p = {0: slice(1, 3), 1: slice(0, 1), -1: slice(3, 4)}[sx]
        else:
            src_p = slice(1, 2)
            dst_p = {0: slice(1, 2), 1: slice(0, 1), -1: slice(2, 3)}[sx]
        src_r = {0: own, 1: slice(rows, rows + H), -1: slice(H, 2 * H)}[sy]
        dst_r = {0: own, 1: slice(0, H), -1: slice(H + rows, ext)}[sy]
        return pltpu.make_async_remote_copy(
            src_ref=ref.at[lead + (every, src_p, src_r)],
            dst_ref=ref.at[lead + (every, dst_p, dst_r)],
            send_sem=send.at[round_id, way],
            recv_sem=recv.at[round_id, way],
            device_id=(gx + sx, gy + sy),
            device_id_type=pl.DeviceIdType.MESH,
        )

    started = []

    def start(ref, lead, kind, round_id, ways):
        for way in ways:
            started.append((ref, lead, kind, round_id, way))

            @pl.when(exists(*DIRS[way]))
            def _(way=way):
                message(ref, lead, kind, round_id, way).start()

    def arrive(ref, lead, kind, round_id, ways):
        for way in ways:
            sx, sy = DIRS[way]

            @pl.when(exists(-sx, -sy))
            def _(way=way):
                message(ref, lead, kind, round_id, way).wait_recv()

    ALL = range(8)
    STAR = range(6)
    start(coef, (), "coef", 0, ALL)
    start(rhs, (), "fine", 1, ALL)

    def lane_of(count):
        return lax.broadcasted_iota(jnp.int32, (count, lanes), 1)

    def make_zshift(count, dist):
        lane = lane_of(count)

        def up(a):
            return jnp.where(lane >= lanes - dist, 0.0, pltpu.roll(a, lanes - dist, 1))

        def down(a):
            return jnp.where(lane < dist, 0.0, pltpu.roll(a, dist, 1))

        return up, down

    def coef_at(which, plane, first, count):
        return coef[which, plane, first : first + count, :]

    def operate(load, plane, first, count):
        up, down = make_zshift(count, 1)

        def mu(dp, dy):
            return coef_at(0, plane + 1 + dp, first + dy, count)

        def lam(dp, dy):
            return coef_at(1, plane + 1 + dp, first + dy, count)

        m0 = mu(0, 0)
        faces = [
            0.5 * (m0 + mu(1, 0)),
            0.5 * (m0 + mu(-1, 0)),
            0.5 * (m0 + mu(0, 1)),
            0.5 * (m0 + mu(0, -1)),
            0.5 * (m0 + up(m0)),
            0.5 * (m0 + down(m0)),
        ]
        centre = [load(c, plane, 0, 0) for c in range(3)]
        vx_up = load(0, plane, 1, 0)
        vy_up = load(1, plane, 0, 1)
        vz_up = up(centre[2])
        here = lam(0, 0) * (
            (vx_up - centre[0]) + (vy_up - centre[1]) + (vz_up - centre[2])
        )
        vx_low = load(0, plane, -1, 0)
        vy_side = load(1, plane, -1, 0)
        vz_side = load(2, plane, -1, 0)
        back_x = lam(-1, 0) * (
            (centre[0] - vx_low)
            + (load(1, plane, -1, 1) - vy_side)
            + (up(vz_side) - vz_side)
        )
        vx_below = load(0, plane, 0, -1)
        vy_low = load(1, plane, 0, -1)
        vz_below = load(2, plane, 0, -1)
        back_y = lam(0, -1) * (
            (load(0, plane, 1, -1) - vx_below)
            + (centre[1] - vy_low)
            + (up(vz_below) - vz_below)
        )
        backs = [back_x, back_y, down(here)]
        out = []
        for c in range(3):
            v = centre[c]
            laplace = (
                faces[0] * ((vx_up if c == 0 else load(c, plane, 1, 0)) - v)
                - faces[1] * (v - load(c, plane, -1, 0))
                + faces[2] * ((vy_up if c == 1 else load(c, plane, 0, 1)) - v)
                - faces[3] * (v - load(c, plane, 0, -1))
                + faces[4] * ((vz_up if c == 2 else up(v)) - v)
                - faces[5] * (v - down(v))
            )
            out.append(-laplace - (here - backs[c]))
        return out

    def direction_load(k, first, count):
        def load(c, plane, dp, dy):
            return dirs[k, c, plane + dp, first + dy : first + dy + count, :]

        return load

    steps = weights(SWEEPS)

    arrive(coef, (), "coef", 0, ALL)
    wide_first, wide = H - 1, rows + 2
    up, down = make_zshift(wide, 1)
    row_id = lax.broadcasted_iota(jnp.int32, (wide, lanes), 0)
    row_ok = jnp.logical_and(
        jnp.logical_or(row_id > 0, gy > 0), jnp.logical_or(row_id < wide - 1, gy < n_gy - 1)
    )
    for plane in range(4):
        m0 = coef_at(0, plane + 1, wide_first, wide)
        l0 = coef_at(1, plane + 1, wide_first, wide)
        total = (
            0.5 * (m0 + coef_at(0, plane + 2, wide_first, wide))
            + 0.5 * (m0 + coef_at(0, plane, wide_first, wide))
            + 0.5 * (m0 + coef_at(0, plane + 1, wide_first + 1, wide))
            + 0.5 * (m0 + coef_at(0, plane + 1, wide_first - 1, wide))
            + 0.5 * (m0 + up(m0))
            + 0.5 * (m0 + down(m0))
            + l0
        )
        sides = (
            coef_at(1, plane, wide_first, wide),
            coef_at(1, plane + 1, wide_first - 1, wide),
            down(l0),
        )
        ok = row_ok
        if plane == 0:
            ok = jnp.logical_and(ok, gx > 0)
        if plane == 3:
            ok = jnp.logical_and(ok, gx < n_gx - 1)
        for c in range(3):
            inv[c, plane, wide_first : wide_first + wide, :] = jnp.where(
                ok, 1.0 / (total + sides[c]), 0.0
            )
    arrive(rhs, (), "fine", 1, ALL)
    wide_rows = slice(wide_first, wide_first + wide)
    for plane in range(4):
        for c in range(3):
            dirs[0, c, plane, wide_rows, :] = (
                steps[0][1] * inv[c, plane, wide_rows, :] * rhs[c, plane, wide_rows, :]
            )

    def relax(k, source, target, following):
        for plane in (1, 2):
            applied = operate(direction_load(k, H, rows), plane, H, rows)
            for c in range(3):
                left = source(c, plane) - applied[c]
                target(c, plane, left)
                if following is not None:
                    dirs[k + 1, c, plane, own, :] = (
                        following[0] * dirs[k, c, plane, own, :]
                        + following[1] * (inv[c, plane, own, :] * left)
                    )

    def into_rbuf(c, plane, value):
        rbuf[c, plane, own, :] = value

    def from_rbuf(c, plane):
        return rbuf[c, plane, own, :]

    relax(0, lambda c, plane: rhs[c, plane, own, :], into_rbuf, steps[1])
    start(dirs, (1,), "fine", 2, STAR)

    lane = lane_of(ext)
    rid = lax.broadcasted_iota(jnp.int32, (ext, lanes), 0)
    lane_even = lane % 2 == 0
    row_even = rid % 2 == 0

    def cube_sum(a):
        a = a + jnp.where(lane_even, pltpu.roll(a, lanes - 1, 1), pltpu.roll(a, 1, 1))
        return a + jnp.where(row_even, pltpu.roll(a, ext - 1, 0), pltpu.roll(a, 1, 0))

    labels = []
    label = jnp.int32(0)
    for j in range(n_gy):
        if j > 0:
            label = label + starts_ref[0, j]
        labels.append(label)
    mine = labels[0]
    before = labels[0] - 1
    after = labels[0] - 1
    for j in range(n_gy):
        mine = jnp.where(gy == j, labels[j], mine)
        if j > 0:
            before = jnp.where(gy == j, labels[j - 1], before)
        if j < n_gy - 1:
            after = jnp.where(gy == j, labels[j + 1], after)
    low_open = jnp.logical_and(gy > 0, before == mine)
    high_open = jnp.logical_and(gy < n_gy - 1, after == mine)
    inside = jnp.logical_and(
        jnp.logical_or(rid >= H, low_open), jnp.logical_or(rid < H + rows, high_open)
    )
    up2, down2 = make_zshift(ext, 2)

    def row_up(a):
        return pltpu.roll(a, ext - 2, 0)

    def row_down(a):
        return pltpu.roll(a, 2, 0)

    cmu = jnp.where(inside, 0.125 * cube_sum(coef[0, 2] + coef[0, 3]), 0.0)
    clam = jnp.where(inside, 0.125 * cube_sum(coef[1, 2] + coef[1, 3]), 0.0)
    cf = [
        0.5 * (cmu + row_up(cmu)),
        0.5 * (cmu + row_down(cmu)),
        0.5 * (cmu + up2(cmu)),
        0.5 * (cmu + down2(cmu)),
    ]
    csum = cmu + cf[0] + cf[1] + cf[2] + cf[3]
    cinv = [
        jnp.where(inside, 1.0 / (4.0 * (csum + clam + side)), 0.0)
        for side in (0.0, row_down(clam), down2(clam))
    ]

    def coarse_operate(v):
        vy_up = row_up(v[1])
        vz_up = up2(v[2])
        here = clam * ((vy_up - v[1]) + (vz_up - v[2]) - v[0])
        backs = [0.0, row_down(here), down2(here)]
        out = []
        for c in range(3):
            laplace = (
                cf[0] * ((vy_up if c == 1 else row_up(v[c])) - v[c])
                - cf[1] * (v[c] - row_down(v[c]))
                + cf[2] * ((vz_up if c == 2 else up2(v[c])) - v[c])
                - cf[3] * (v[c] - down2(v[c]))
                - cmu * v[c]
            )
            out.append(4.0 * (-laplace - (here - backs[c])))
        return out

    for c in range(3):
        for plane in (1, 2):
            sol_ref[c, plane - 1] = dirs[0, c, plane, own, :] + dirs[1, c, plane, own, :]
    arrive(dirs, (1,), "fine", 2, STAR)
    relax(1, from_rbuf, into_rbuf, steps[2])
    start(dirs, (2,), "fine", 3, STAR)
    for c in range(3):
        for plane in (1, 2):
            sol_ref[c, plane - 1] += dirs[2, c, plane, own, :]
    arrive(dirs, (2,), "fine", 3, STAR)
    relax(2, from_rbuf, into_rbuf, None)
    start(rbuf, (), "fine", 4, (2, 3, 0, 1, 4, 5, 6, 7))

    sub = lax.broadcasted_iota(jnp.int32, (8, lanes), 0)
    part = jnp.zeros((8, lanes), jnp.float32)
    for c in range(3):
        both = rbuf[c, 1, own, :] + rbuf[c, 2, own, :]
        part = jnp.where(sub == c, jnp.sum(both, axis=0, keepdims=True), part)
    sums[0] = part

    def sum_message(step):
        return pltpu.make_async_remote_copy(
            src_ref=sums.at[0],
            dst_ref=sums.at[step],
            send_sem=sum_send.at[step],
            recv_sem=sum_recv.at[step],
            device_id=(gx, lax.rem(gy + step, n_gy)),
            device_id_type=pl.DeviceIdType.MESH,
        )

    for step in range(1, n_gy):
        sum_message(step).start()

    arrive(rbuf, (), "fine", 4, (2, 3))
    left = [
        jnp.where(inside, cube_sum(rbuf[c, 1] + rbuf[c, 2]), 0.0) for c in range(3)
    ]
    coarse_steps = weights(COARSE_SWEEPS)
    direction = [coarse_steps[0][1] * cinv[c] * left[c] for c in range(3)]
    smoothed = direction
    for old, new in coarse_steps[1:]:
        applied = coarse_operate(direction)
        left = [left[c] - applied[c] for c in range(3)]
        direction = [old * direction[c] + new * (cinv[c] * left[c]) for c in range(3)]
        smoothed = [smoothed[c] + direction[c] for c in range(3)]

    total = sums[0]
    members = jnp.float32(1.0)
    for step in range(1, n_gy):
        sum_message(step).wait_recv()
        source = lax.rem(gy + n_gy - step, n_gy)
        other = labels[0]
        for j in range(1, n_gy):
            other = jnp.where(source == j, labels[j], other)
        same = jnp.where(other == mine, jnp.float32(1.0), jnp.float32(0.0))
        total = total + same * sums[step]
        members = members + same
    cells_dev = (rows // 2) * (lanes // 2)
    scale = jnp.full((8, 1), SHIFT_SCALE * cells_dev, jnp.float32) * members
    shift = jnp.sum(total, axis=1, keepdims=True) / scale
    for c in range(3):
        fc[c, 1, own, :] = smoothed[c][H : H + rows] + shift[c : c + 1, :]
    start(fc, (), "coarse", 5, ALL)
    for c in range(3):
        for plane in (1, 2):
            sol_ref[c, plane - 1] += fc[c, 1, own, :]
    arrive(rbuf, (), "fine", 4, (0, 1, 4, 5, 6, 7))
    arrive(fc, (), "coarse", 5, ALL)

    def fc_load(c, plane, dp, dy):
        return fc[c, (plane + 1 + dp) // 2, wide_first + dy : wide_first + dy + wide, :]

    for plane in range(4):
        applied = operate(fc_load, plane, wide_first, wide)
        for c in range(3):
            value = rbuf[c, plane, wide_rows, :] - applied[c]
            r2buf[c, plane, wide_rows, :] = value
            dirs[3, c, plane, wide_rows, :] = steps[0][1] * inv[c, plane, wide_rows, :] * value

    def into_r2(c, plane, value):
        r2buf[c, plane, own, :] = value

    def from_r2(c, plane):
        return r2buf[c, plane, own, :]

    def into_result(c, plane, value):
        res_ref[c, plane - 1] = value

    relax(3, from_r2, into_r2, steps[1])
    start(dirs, (4,), "fine", 6, STAR)
    for c in range(3):
        for plane in (1, 2):
            sol_ref[c, plane - 1] += dirs[3, c, plane, own, :] + dirs[4, c, plane, own, :]
    arrive(dirs, (4,), "fine", 6, STAR)
    relax(4, from_r2, into_r2, steps[2])
    start(dirs, (5,), "fine", 7, STAR)
    for c in range(3):
        for plane in (1, 2):
            sol_ref[c, plane - 1] += dirs[5, c, plane, own, :]
    arrive(dirs, (5,), "fine", 7, STAR)
    relax(5, from_r2, into_result, None)

    for ref, lead, kind, round_id, way in started:

        @pl.when(exists(*DIRS[way]))
        def _(ref=ref, lead=lead, kind=kind, round_id=round_id, way=way):
            message(ref, lead, kind, round_id, way).wait_send()

    for step in range(1, n_gy):
        sum_message(step).wait_send()


def solution(mesh):
    n_gx = mesh.shape["gx"]
    n_gy = mesh.shape["gy"]

    def shards(rhs_field, shear_modulus, lame_lambda, group_start):
        _, planes, rows, lanes = rhs_field.shape
        assert planes == 2
        ext = rows + 2 * H
        vmem = pl.BlockSpec(memory_space=pltpu.VMEM)
        hbm = pl.BlockSpec(memory_space=pltpu.MemorySpace.HBM)
        field = jax.ShapeDtypeStruct(rhs_field.shape, jnp.float32)
        f32 = jnp.float32
        return pl.pallas_call(
            functools.partial(kernel, n_gx, n_gy),
            out_shape=(field, field),
            in_specs=[hbm, hbm, hbm, hbm],
            out_specs=(vmem, vmem),
            scratch_shapes=[
                pltpu.VMEM((2, 6, ext, lanes), f32),
                pltpu.VMEM((3, 4, ext, lanes), f32),
                pltpu.VMEM((3, 4, ext, lanes), f32),
                pltpu.VMEM((6, 3, 4, ext, lanes), f32),
                pltpu.VMEM((3, 4, ext, lanes), f32),
                pltpu.VMEM((3, 4, ext, lanes), f32),
                pltpu.VMEM((3, 3, ext, lanes), f32),
                pltpu.VMEM((n_gy, 8, lanes), f32),
                pltpu.SMEM((1, n_gy), jnp.int32),
                pltpu.SemaphoreType.DMA((8, 8)),
                pltpu.SemaphoreType.DMA((8, 8)),
                pltpu.SemaphoreType.DMA((n_gy,)),
                pltpu.SemaphoreType.DMA((n_gy,)),
                pltpu.SemaphoreType.DMA((4,)),
            ],
            compiler_params=pltpu.CompilerParams(
                collective_id=0, has_side_effects=True
            ),
            cost_estimate=pl.CostEstimate(
                flops=10_000_000, bytes_accessed=400_000, transcendentals=0
            ),
        )(rhs_field, shear_modulus, lame_lambda, group_start)

    return jax.shard_map(
        shards,
        mesh=mesh,
        in_specs=(
            P(None, "gx", "gy", None),
            P("gx", "gy", None),
            P("gx", "gy", None),
            P("gx", None),
        ),
        out_specs=(P(None, "gx", "gy", None), P(None, "gx", "gy", None)),
        check_vma=False,
    )
```

```python
import functools

import jax
import jax.numpy as jnp
from jax import lax
from jax.experimental import pallas as pl
from jax.experimental.pallas import tpu as pltpu
from jax.sharding import PartitionSpec as P

SWEEPS = 3
COARSE_SWEEPS = 4
LOW_BOUND = 0.5
HIGH_BOUND = 6.0
SHIFT_SCALE = 48.0

MID = 0.5 * (HIGH_BOUND + LOW_BOUND)
HALF = 0.5 * (HIGH_BOUND - LOW_BOUND)
SIGMA = MID / HALF

H = 8
DIRS = ((1, 0), (-1, 0), (0, 1), (0, -1), (1, -1), (-1, 1), (1, 1), (-1, -1))


def weights(steps):
    out = [(0.0, 1.0 / MID)]
    old = 1.0 / SIGMA
    for _ in range(steps - 1):
        new = 1.0 / (2.0 * SIGMA - old)
        out.append((new * old, 2.0 * new / HALF))
        old = new
    return out


def kernel(
    n_gx, n_gy, rhs_in, mu_in, lam_in, starts_in, sol_ref, res_ref,
    coef, rhs, inv, dirs, rbuf, r2buf, fc, sums, starts_ref, send, recv, sum_send, sum_recv, load_sem,
):
    rows = rhs_in.shape[2]
    lanes = rhs_in.shape[3]
    ext = rows + 2 * H
    gx = lax.axis_index("gx")
    gy = lax.axis_index("gy")
    own = slice(H, H + rows)

    def exists(sx, sy):
        ok = None
        for pos, step, count in ((gx, sx, n_gx), (gy, sy, n_gy)):
            if step == 1:
                here = pos < count - 1
            elif step == -1:
                here = pos > 0
            else:
                continue
            ok = here if ok is None else jnp.logical_and(ok, here)
        return ok

    barrier = pltpu.get_barrier_semaphore()
    expected = jnp.int32(n_gy - 1)
    for sx, sy in DIRS:
        if sx == 0:
            continue

        @pl.when(exists(sx, sy))
        def _(sx=sx, sy=sy):
            pl.semaphore_signal(
                barrier, inc=1, device_id=(gx + sx, gy + sy), device_id_type=pl.DeviceIdType.MESH
            )

        expected = expected + exists(sx, sy).astype(jnp.int32)
    for step in range(1, n_gy):
        pl.semaphore_signal(
            barrier,
            inc=1,
            device_id=(gx, lax.rem(gy + step, n_gy)),
            device_id_type=pl.DeviceIdType.MESH,
        )
    loads = [
        pltpu.make_async_copy(source, target, load_sem.at[k])
        for k, (source, target) in enumerate(
            (
                (mu_in, coef.at[0, 2:4, own]),
                (lam_in, coef.at[1, 2:4, own]),
                (rhs_in, rhs.at[:, 1:3, own]),
                (starts_in, starts_ref),
            )
        )
    ]
    for copy in loads:
        copy.start()

    def clear(ref, index):
        ref[index] = jnp.zeros_like(ref[index])

    every = slice(None)
    for edge, planes2, planes1, planef in (
        (gx == 0, slice(0, 2), 0, 0),
        (gx == n_gx - 1, slice(4, 6), 3, 2),
    ):

        @pl.when(edge)
        def _(planes2=planes2, planes1=planes1, planef=planef):
            clear(coef, (every, planes2))
            clear(rhs, (every, planes1))
            clear(rbuf, (every, planes1))
            clear(fc, (every, planef))
            for k in (1, 2, 4, 5):
                clear(dirs, (k, every, planes1))

    for edge, edge_rows in ((gy == 0, slice(0, H)), (gy == n_gy - 1, slice(H + rows, ext))):

        @pl.when(edge)
        def _(edge_rows=edge_rows):
            for ref in (coef, rhs, rbuf, fc):
                clear(ref, (every, every, edge_rows))
            for k in (1, 2, 4, 5):
                clear(dirs, (k, every, every, edge_rows))

    for copy in loads:
        copy.wait()
    pl.semaphore_wait(barrier, expected)

    def message(ref, lead, kind, round_id, way):
        sx, sy = DIRS[way]
        if kind == "coef":
            src_p = slice(2, 4)
            dst_p = {0: slice(2, 4), 1: slice(0, 2), -1: slice(4, 6)}[sx]
        elif kind == "fine":
            src_p = {0: slice(1, 3), 1: slice(2, 3), -1: slice(1, 2)}[sx]
            dst_p = {0: slice(1, 3), 1: slice(0, 1), -1: slice(3, 4)}[sx]
        else:
            src_p = slice(1, 2)
            dst_p = {0: slice(1, 2), 1: slice(0, 1), -1: slice(2, 3)}[sx]
        src_r = {0: own, 1: slice(rows, rows + H), -1: slice(H, 2 * H)}[sy]
        dst_r = {0: own, 1: slice(0, H), -1: slice(H + rows, ext)}[sy]
        return pltpu.make_async_remote_copy(
            src_ref=ref.at[lead + (every, src_p, src_r)],
            dst_ref=ref.at[lead + (every, dst_p, dst_r)],
            send_sem=send.at[round_id, way],
            recv_sem=recv.at[round_id, way],
            device_id=(gx + sx, gy + sy),
            device_id_type=pl.DeviceIdType.MESH,
        )

    started = []

    def start(ref, lead, kind, round_id, ways):
        for way in ways:
            started.append((ref, lead, kind, round_id, way))

            @pl.when(exists(*DIRS[way]))
            def _(way=way):
                message(ref, lead, kind, round_id, way).start()

    def arrive(ref, lead, kind, round_id, ways):
        for way in ways:
            sx, sy = DIRS[way]

            @pl.when(exists(-sx, -sy))
            def _(way=way):
                message(ref, lead, kind, round_id, way).wait_recv()

    ALL = range(8)
    STAR = range(6)
    start(coef, (), "coef", 0, ALL)
    start(rhs, (), "fine", 1, ALL)

    def lane_of(count):
        return lax.broadcasted_iota(jnp.int32, (count, lanes), 1)

    def make_zshift(count, dist):
        lane = lane_of(count)

        def up(a):
            return jnp.where(lane >= lanes - dist, 0.0, pltpu.roll(a, lanes - dist, 1))

        def down(a):
            return jnp.where(lane < dist, 0.0, pltpu.roll(a, dist, 1))

        return up, down

    def coef_at(which, plane, first, count):
        return coef[which, plane, first : first + count, :]

    def operate(load, plane, first, count):
        up, down = make_zshift(count, 1)

        def mu(dp, dy):
            return coef_at(0, plane + 1 + dp, first + dy, count)

        def lam(dp, dy):
            return coef_at(1, plane + 1 + dp, first + dy, count)

        m0 = mu(0, 0)
        faces = [
            0.5 * (m0 + mu(1, 0)),
            0.5 * (m0 + mu(-1, 0)),
            0.5 * (m0 + mu(0, 1)),
            0.5 * (m0 + mu(0, -1)),
            0.5 * (m0 + up(m0)),
            0.5 * (m0 + down(m0)),
        ]
        centre = [load(c, plane, 0, 0) for c in range(3)]
        vx_up = load(0, plane, 1, 0)
        vy_up = load(1, plane, 0, 1)
        vz_up = up(centre[2])
        here = lam(0, 0) * (
            (vx_up - centre[0]) + (vy_up - centre[1]) + (vz_up - centre[2])
        )
        vx_low = load(0, plane, -1, 0)
        vy_side = load(1, plane, -1, 0)
        vz_side = load(2, plane, -1, 0)
        back_x = lam(-1, 0) * (
            (centre[0] - vx_low)
            + (load(1, plane, -1, 1) - vy_side)
            + (up(vz_side) - vz_side)
        )
        vx_below = load(0, plane, 0, -1)
        vy_low = load(1, plane, 0, -1)
        vz_below = load(2, plane, 0, -1)
        back_y = lam(0, -1) * (
            (load(0, plane, 1, -1) - vx_below)
            + (centre[1] - vy_low)
            + (up(vz_below) - vz_below)
        )
        backs = [back_x, back_y, down(here)]
        out = []
        for c in range(3):
            v = centre[c]
            laplace = (
                faces[0] * ((vx_up if c == 0 else load(c, plane, 1, 0)) - v)
                - faces[1] * (v - load(c, plane, -1, 0))
                + faces[2] * ((vy_up if c == 1 else load(c, plane, 0, 1)) - v)
                - faces[3] * (v - load(c, plane, 0, -1))
                + faces[4] * ((vz_up if c == 2 else up(v)) - v)
                - faces[5] * (v - down(v))
            )
            out.append(-laplace - (here - backs[c]))
        return out

    def direction_load(k, first, count):
        def load(c, plane, dp, dy):
            return dirs[k, c, plane + dp, first + dy : first + dy + count, :]

        return load

    steps = weights(SWEEPS)

    arrive(coef, (), "coef", 0, ALL)
    wide_first, wide = H - 1, rows + 2
    up, down = make_zshift(wide, 1)
    row_id = lax.broadcasted_iota(jnp.int32, (wide, lanes), 0)
    row_ok = jnp.logical_and(
        jnp.logical_or(row_id > 0, gy > 0), jnp.logical_or(row_id < wide - 1, gy < n_gy - 1)
    )
    for plane in range(4):
        m0 = coef_at(0, plane + 1, wide_first, wide)
        l0 = coef_at(1, plane + 1, wide_first, wide)
        total = (
            0.5 * (m0 + coef_at(0, plane + 2, wide_first, wide))
            + 0.5 * (m0 + coef_at(0, plane, wide_first, wide))
            + 0.5 * (m0 + coef_at(0, plane + 1, wide_first + 1, wide))
            + 0.5 * (m0 + coef_at(0, plane + 1, wide_first - 1, wide))
            + 0.5 * (m0 + up(m0))
            + 0.5 * (m0 + down(m0))
            + l0
        )
        sides = (
            coef_at(1, plane, wide_first, wide),
            coef_at(1, plane + 1, wide_first - 1, wide),
            down(l0),
        )
        ok = row_ok
        if plane == 0:
            ok = jnp.logical_and(ok, gx > 0)
        if plane == 3:
            ok = jnp.logical_and(ok, gx < n_gx - 1)
        for c in range(3):
            inv[c, plane, wide_first : wide_first + wide, :] = jnp.where(
                ok, 1.0 / (total + sides[c]), 0.0
            )
    arrive(rhs, (), "fine", 1, ALL)
    wide_rows = slice(wide_first, wide_first + wide)
    for plane in range(4):
        for c in range(3):
            dirs[0, c, plane, wide_rows, :] = (
                steps[0][1] * inv[c, plane, wide_rows, :] * rhs[c, plane, wide_rows, :]
            )

    def relax(k, source, target, following):
        for plane in (1, 2):
            applied = operate(direction_load(k, H, rows), plane, H, rows)
            for c in range(3):
                left = source(c, plane) - applied[c]
                target(c, plane, left)
                if following is not None:
                    dirs[k + 1, c, plane, own, :] = (
                        following[0] * dirs[k, c, plane, own, :]
                        + following[1] * (inv[c, plane, own, :] * left)
                    )

    def into_rbuf(c, plane, value):
        rbuf[c, plane, own, :] = value

    def from_rbuf(c, plane):
        return rbuf[c, plane, own, :]

    relax(0, lambda c, plane: rhs[c, plane, own, :], into_rbuf, steps[1])
    start(dirs, (1,), "fine", 2, STAR)

    lane = lane_of(ext)
    rid = lax.broadcasted_iota(jnp.int32, (ext, lanes), 0)
    lane_even = lane % 2 == 0
    row_even = rid % 2 == 0

    def cube_sum(a):
        a = a + jnp.where(lane_even, pltpu.roll(a, lanes - 1, 1), pltpu.roll(a, 1, 1))
        return a + jnp.where(row_even, pltpu.roll(a, ext - 1, 0), pltpu.roll(a, 1, 0))

    labels = []
    label = jnp.int32(0)
    for j in range(n_gy):
        if j > 0:
            label = label + starts_ref[0, j]
        labels.append(label)
    mine = labels[0]
    before = labels[0] - 1
    after = labels[0] - 1
    for j in range(n_gy):
        mine = jnp.where(gy == j, labels[j], mine)
        if j > 0:
            before = jnp.where(gy == j, labels[j - 1], before)
        if j < n_gy - 1:
            after = jnp.where(gy == j, labels[j + 1], after)
    low_open = jnp.logical_and(gy > 0, before == mine)
    high_open = jnp.logical_and(gy < n_gy - 1, after == mine)
    inside = jnp.logical_and(
        jnp.logical_or(rid >= H, low_open), jnp.logical_or(rid < H + rows, high_open)
    )
    up2, down2 = make_zshift(ext, 2)

    def row_up(a):
        return pltpu.roll(a, ext - 2, 0)

    def row_down(a):
        return pltpu.roll(a, 2, 0)

    cmu = jnp.where(inside, 0.125 * cube_sum(coef[0, 2] + coef[0, 3]), 0.0)
    clam = jnp.where(inside, 0.125 * cube_sum(coef[1, 2] + coef[1, 3]), 0.0)
    cf = [
        0.5 * (cmu + row_up(cmu)),
        0.5 * (cmu + row_down(cmu)),
        0.5 * (cmu + up2(cmu)),
        0.5 * (cmu + down2(cmu)),
    ]
    csum = cmu + cf[0] + cf[1] + cf[2] + cf[3]
    cinv = [
        jnp.where(inside, 1.0 / (4.0 * (csum + clam + side)), 0.0)
        for side in (0.0, row_down(clam), down2(clam))
    ]

    def coarse_operate(v):
        vy_up = row_up(v[1])
        vz_up = up2(v[2])
        here = clam * ((vy_up - v[1]) + (vz_up - v[2]) - v[0])
        backs = [0.0, row_down(here), down2(here)]
        out = []
        for c in range(3):
            laplace = (
                cf[0] * ((vy_up if c == 1 else row_up(v[c])) - v[c])
                - cf[1] * (v[c] - row_down(v[c]))
                + cf[2] * ((vz_up if c == 2 else up2(v[c])) - v[c])
                - cf[3] * (v[c] - down2(v[c]))
                - cmu * v[c]
            )
            out.append(4.0 * (-laplace - (here - backs[c])))
        return out

    for c in range(3):
        for plane in (1, 2):
            sol_ref[c, plane - 1] = dirs[0, c, plane, own, :] + dirs[1, c, plane, own, :]
    arrive(dirs, (1,), "fine", 2, STAR)
    relax(1, from_rbuf, into_rbuf, steps[2])
    start(dirs, (2,), "fine", 3, STAR)
    for c in range(3):
        for plane in (1, 2):
            sol_ref[c, plane - 1] += dirs[2, c, plane, own, :]
    arrive(dirs, (2,), "fine", 3, STAR)
    relax(2, from_rbuf, into_rbuf, None)
    start(rbuf, (), "fine", 4, (2, 3, 0, 1, 4, 5, 6, 7))

    sub = lax.broadcasted_iota(jnp.int32, (8, lanes), 0)
    part = jnp.zeros((8, lanes), jnp.float32)
    for c in range(3):
        both = rbuf[c, 1, own, :] + rbuf[c, 2, own, :]
        part = jnp.where(sub == c, jnp.sum(both, axis=0, keepdims=True), part)
    sums[0] = part

    def sum_message(step):
        return pltpu.make_async_remote_copy(
            src_ref=sums.at[0],
            dst_ref=sums.at[step],
            send_sem=sum_send.at[step],
            recv_sem=sum_recv.at[step],
            device_id=(gx, lax.rem(gy + step, n_gy)),
            device_id_type=pl.DeviceIdType.MESH,
        )

    for step in range(1, n_gy):
        sum_message(step).start()

    arrive(rbuf, (), "fine", 4, (2, 3))
    left = [
        jnp.where(inside, cube_sum(rbuf[c, 1] + rbuf[c, 2]), 0.0) for c in range(3)
    ]
    coarse_steps = weights(COARSE_SWEEPS)
    direction = [coarse_steps[0][1] * cinv[c] * left[c] for c in range(3)]
    smoothed = direction
    for old, new in coarse_steps[1:]:
        applied = coarse_operate(direction)
        left = [left[c] - applied[c] for c in range(3)]
        direction = [old * direction[c] + new * (cinv[c] * left[c]) for c in range(3)]
        smoothed = [smoothed[c] + direction[c] for c in range(3)]

    total = sums[0]
    members = jnp.float32(1.0)
    for step in range(1, n_gy):
        sum_message(step).wait_recv()
        source = lax.rem(gy + n_gy - step, n_gy)
        other = labels[0]
        for j in range(1, n_gy):
            other = jnp.where(source == j, labels[j], other)
        same = jnp.where(other == mine, jnp.float32(1.0), jnp.float32(0.0))
        total = total + same * sums[step]
        members = members + same
    cells_dev = (rows // 2) * (lanes // 2)
    scale = jnp.full((8, 1), SHIFT_SCALE * cells_dev, jnp.float32) * members
    shift = jnp.sum(total, axis=1, keepdims=True) / scale
    for c in range(3):
        fc[c, 1, own, :] = smoothed[c][H : H + rows] + shift[c : c + 1, :]
    start(fc, (), "coarse", 5, ALL)
    for c in range(3):
        for plane in (1, 2):
            sol_ref[c, plane - 1] += fc[c, 1, own, :]
    arrive(rbuf, (), "fine", 4, (0, 1, 4, 5, 6, 7))
    arrive(fc, (), "coarse", 5, ALL)

    def fc_load(c, plane, dp, dy):
        return fc[c, (plane + 1 + dp) // 2, wide_first + dy : wide_first + dy + wide, :]

    for plane in range(4):
        applied = operate(fc_load, plane, wide_first, wide)
        for c in range(3):
            value = rbuf[c, plane, wide_rows, :] - applied[c]
            r2buf[c, plane, wide_rows, :] = value
            dirs[3, c, plane, wide_rows, :] = steps[0][1] * inv[c, plane, wide_rows, :] * value

    def into_r2(c, plane, value):
        r2buf[c, plane, own, :] = value

    def from_r2(c, plane):
        return r2buf[c, plane, own, :]

    def into_result(c, plane, value):
        res_ref[c, plane - 1] = value

    relax(3, from_r2, into_r2, steps[1])
    start(dirs, (4,), "fine", 6, STAR)
    for c in range(3):
        for plane in (1, 2):
            sol_ref[c, plane - 1] += dirs[3, c, plane, own, :] + dirs[4, c, plane, own, :]
    arrive(dirs, (4,), "fine", 6, STAR)
    relax(4, from_r2, into_r2, steps[2])
    start(dirs, (5,), "fine", 7, STAR)
    for c in range(3):
        for plane in (1, 2):
            sol_ref[c, plane - 1] += dirs[5, c, plane, own, :]
    for ref, lead, kind, round_id, way in started:

        @pl.when(exists(*DIRS[way]))
        def _(ref=ref, lead=lead, kind=kind, round_id=round_id, way=way):
            message(ref, lead, kind, round_id, way).wait_send()

    for step in range(1, n_gy):
        sum_message(step).wait_send()

    arrive(dirs, (5,), "fine", 7, STAR)
    relax(5, from_r2, into_result, None)


def solution(mesh):
    n_gx = mesh.shape["gx"]
    n_gy = mesh.shape["gy"]

    def shards(rhs_field, shear_modulus, lame_lambda, group_start):
        _, planes, rows, lanes = rhs_field.shape
        assert planes == 2
        ext = rows + 2 * H
        vmem = pl.BlockSpec(memory_space=pltpu.VMEM)
        hbm = pl.BlockSpec(memory_space=pltpu.MemorySpace.HBM)
        field = jax.ShapeDtypeStruct(rhs_field.shape, jnp.float32)
        f32 = jnp.float32
        return pl.pallas_call(
            functools.partial(kernel, n_gx, n_gy),
            out_shape=(field, field),
            in_specs=[hbm, hbm, hbm, hbm],
            out_specs=(vmem, vmem),
            scratch_shapes=[
                pltpu.VMEM((2, 6, ext, lanes), f32),
                pltpu.VMEM((3, 4, ext, lanes), f32),
                pltpu.VMEM((3, 4, ext, lanes), f32),
                pltpu.VMEM((6, 3, 4, ext, lanes), f32),
                pltpu.VMEM((3, 4, ext, lanes), f32),
                pltpu.VMEM((3, 4, ext, lanes), f32),
                pltpu.VMEM((3, 3, ext, lanes), f32),
                pltpu.VMEM((n_gy, 8, lanes), f32),
                pltpu.SMEM((1, n_gy), jnp.int32),
                pltpu.SemaphoreType.DMA((8, 8)),
                pltpu.SemaphoreType.DMA((8, 8)),
                pltpu.SemaphoreType.DMA((n_gy,)),
                pltpu.SemaphoreType.DMA((n_gy,)),
                pltpu.SemaphoreType.DMA((4,)),
            ],
            compiler_params=pltpu.CompilerParams(
                collective_id=0, has_side_effects=True
            ),
            cost_estimate=pl.CostEstimate(
                flops=10_000_000, bytes_accessed=400_000, transcendentals=0
            ),
        )(rhs_field, shear_modulus, lame_lambda, group_start)

    return jax.shard_map(
        shards,
        mesh=mesh,
        in_specs=(
            P(None, "gx", "gy", None),
            P("gx", "gy", None),
            P("gx", "gy", None),
            P("gx", None),
        ),
        out_specs=(P(None, "gx", "gy", None), P(None, "gx", "gy", None)),
        check_vma=False,
    )
```

```python
import functools

import jax
import jax.numpy as jnp
from jax import lax
from jax.experimental import pallas as pl
from jax.experimental.pallas import tpu as pltpu
from jax.sharding import PartitionSpec as P

SWEEPS = 3
COARSE_SWEEPS = 4
LOW_BOUND = 0.5
HIGH_BOUND = 6.0
SHIFT_SCALE = 48.0

MID = 0.5 * (HIGH_BOUND + LOW_BOUND)
HALF = 0.5 * (HIGH_BOUND - LOW_BOUND)
SIGMA = MID / HALF

H = 8
DIRS = ((1, 0), (-1, 0), (0, 1), (0, -1), (1, -1), (-1, 1), (1, 1), (-1, -1))


def weights(steps):
    out = [(0.0, 1.0 / MID)]
    old = 1.0 / SIGMA
    for _ in range(steps - 1):
        new = 1.0 / (2.0 * SIGMA - old)
        out.append((new * old, 2.0 * new / HALF))
        old = new
    return out


def kernel(
    n_gx, n_gy, rhs_in, mu_in, lam_in, starts_in, sol_ref, res_ref,
    coef, rhs, inv, dirs, rbuf, r2buf, fc, sums, starts_ref, send, recv, sum_send, sum_recv, load_sem,
):
    rows = rhs_in.shape[2]
    lanes = rhs_in.shape[3]
    ext = rows + 2 * H
    gx = lax.axis_index("gx")
    gy = lax.axis_index("gy")
    own = slice(H, H + rows)

    def exists(sx, sy):
        ok = None
        for pos, step, count in ((gx, sx, n_gx), (gy, sy, n_gy)):
            if step == 1:
                here = pos < count - 1
            elif step == -1:
                here = pos > 0
            else:
                continue
            ok = here if ok is None else jnp.logical_and(ok, here)
        return ok

    barrier = pltpu.get_barrier_semaphore()
    expected = jnp.int32(n_gy - 1)
    for sx, sy in DIRS:
        if sx == 0:
            continue

        @pl.when(exists(sx, sy))
        def _(sx=sx, sy=sy):
            pl.semaphore_signal(
                barrier, inc=1, device_id=(gx + sx, gy + sy), device_id_type=pl.DeviceIdType.MESH
            )

        expected = expected + exists(sx, sy).astype(jnp.int32)
    for step in range(1, n_gy):
        pl.semaphore_signal(
            barrier,
            inc=1,
            device_id=(gx, lax.rem(gy + step, n_gy)),
            device_id_type=pl.DeviceIdType.MESH,
        )
    loads = [
        pltpu.make_async_copy(source, target, load_sem.at[k])
        for k, (source, target) in enumerate(
            (
                (mu_in, coef.at[0, 2:4, own]),
                (lam_in, coef.at[1, 2:4, own]),
                (rhs_in, rhs.at[:, 1:3, own]),
                (starts_in, starts_ref),
            )
        )
    ]
    for copy in loads:
        copy.start()

    def clear(ref, index):
        ref[index] = jnp.zeros_like(ref[index])

    every = slice(None)
    for edge, planes2, planes1, planef in (
        (gx == 0, slice(0, 2), 0, 0),
        (gx == n_gx - 1, slice(4, 6), 3, 2),
    ):

        @pl.when(edge)
        def _(planes2=planes2, planes1=planes1, planef=planef):
            clear(coef, (every, planes2))
            clear(rhs, (every, planes1))
            clear(rbuf, (every, planes1))
            clear(fc, (every, planef))
            for k in (1, 2, 4, 5):
                clear(dirs, (k, every, planes1))

    for edge, edge_rows in ((gy == 0, slice(0, H)), (gy == n_gy - 1, slice(H + rows, ext))):

        @pl.when(edge)
        def _(edge_rows=edge_rows):
            for ref in (coef, rhs, rbuf, fc):
                clear(ref, (every, every, edge_rows))
            for k in (1, 2, 4, 5):
                clear(dirs, (k, every, every, edge_rows))

    for copy in loads:
        copy.wait()
    pl.semaphore_wait(barrier, expected)

    def message(ref, lead, kind, round_id, way):
        sx, sy = DIRS[way]
        if kind == "coef":
            src_p = slice(2, 4)
            dst_p = {0: slice(2, 4), 1: slice(0, 2), -1: slice(4, 6)}[sx]
        elif kind == "fine":
            src_p = {0: slice(1, 3), 1: slice(2, 3), -1: slice(1, 2)}[sx]
            dst_p = {0: slice(1, 3), 1: slice(0, 1), -1: slice(3, 4)}[sx]
        else:
            src_p = slice(1, 2)
            dst_p = {0: slice(1, 2), 1: slice(0, 1), -1: slice(2, 3)}[sx]
        src_r = {0: own, 1: slice(rows, rows + H), -1: slice(H, 2 * H)}[sy]
        dst_r = {0: own, 1: slice(0, H), -1: slice(H + rows, ext)}[sy]
        return pltpu.make_async_remote_copy(
            src_ref=ref.at[lead + (every, src_p, src_r)],
            dst_ref=ref.at[lead + (every, dst_p, dst_r)],
            send_sem=send.at[round_id, way],
            recv_sem=recv.at[round_id, way],
            device_id=(gx + sx, gy + sy),
            device_id_type=pl.DeviceIdType.MESH,
        )

    started = []

    def start(ref, lead, kind, round_id, ways):
        for way in ways:
            started.append((ref, lead, kind, round_id, way))

            @pl.when(exists(*DIRS[way]))
            def _(way=way):
                message(ref, lead, kind, round_id, way).start()

    def arrive(ref, lead, kind, round_id, ways):
        for way in ways:
            sx, sy = DIRS[way]

            @pl.when(exists(-sx, -sy))
            def _(way=way):
                message(ref, lead, kind, round_id, way).wait_recv()

    ALL = range(8)
    STAR = range(6)
    start(coef, (), "coef", 0, ALL)
    start(rhs, (), "fine", 1, ALL)

    def lane_of(count):
        return lax.broadcasted_iota(jnp.int32, (count, lanes), 1)

    def make_zshift(count, dist):
        lane = lane_of(count)

        def up(a):
            return jnp.where(lane >= lanes - dist, 0.0, pltpu.roll(a, lanes - dist, 1))

        def down(a):
            return jnp.where(lane < dist, 0.0, pltpu.roll(a, dist, 1))

        return up, down

    def coef_at(which, plane, first, count):
        return coef[which, plane, first : first + count, :]

    def operate(load, plane, first, count):
        up, down = make_zshift(count, 1)

        def mu(dp, dy):
            return coef_at(0, plane + 1 + dp, first + dy, count)

        def lam(dp, dy):
            return coef_at(1, plane + 1 + dp, first + dy, count)

        m0 = mu(0, 0)
        faces = [
            0.5 * (m0 + mu(1, 0)),
            0.5 * (m0 + mu(-1, 0)),
            0.5 * (m0 + mu(0, 1)),
            0.5 * (m0 + mu(0, -1)),
            0.5 * (m0 + up(m0)),
            0.5 * (m0 + down(m0)),
        ]
        centre = [load(c, plane, 0, 0) for c in range(3)]
        vx_up = load(0, plane, 1, 0)
        vy_up = load(1, plane, 0, 1)
        vz_up = up(centre[2])
        here = lam(0, 0) * (
            (vx_up - centre[0]) + (vy_up - centre[1]) + (vz_up - centre[2])
        )
        vx_low = load(0, plane, -1, 0)
        vy_side = load(1, plane, -1, 0)
        vz_side = load(2, plane, -1, 0)
        back_x = lam(-1, 0) * (
            (centre[0] - vx_low)
            + (load(1, plane, -1, 1) - vy_side)
            + (up(vz_side) - vz_side)
        )
        vx_below = load(0, plane, 0, -1)
        vy_low = load(1, plane, 0, -1)
        vz_below = load(2, plane, 0, -1)
        back_y = lam(0, -1) * (
            (load(0, plane, 1, -1) - vx_below)
            + (centre[1] - vy_low)
            + (up(vz_below) - vz_below)
        )
        backs = [back_x, back_y, down(here)]
        out = []
        for c in range(3):
            v = centre[c]
            laplace = (
                faces[0] * ((vx_up if c == 0 else load(c, plane, 1, 0)) - v)
                - faces[1] * (v - load(c, plane, -1, 0))
                + faces[2] * ((vy_up if c == 1 else load(c, plane, 0, 1)) - v)
                - faces[3] * (v - load(c, plane, 0, -1))
                + faces[4] * ((vz_up if c == 2 else up(v)) - v)
                - faces[5] * (v - down(v))
            )
            out.append(-laplace - (here - backs[c]))
        return out

    def direction_load(k, first, count):
        def load(c, plane, dp, dy):
            return dirs[k, c, plane + dp, first + dy : first + dy + count, :]

        return load

    steps = weights(SWEEPS)

    arrive(coef, (), "coef", 0, ALL)
    wide_first, wide = H - 1, rows + 2
    up, down = make_zshift(wide, 1)
    row_id = lax.broadcasted_iota(jnp.int32, (wide, lanes), 0)
    row_ok = jnp.logical_and(
        jnp.logical_or(row_id > 0, gy > 0), jnp.logical_or(row_id < wide - 1, gy < n_gy - 1)
    )
    for plane in range(4):
        m0 = coef_at(0, plane + 1, wide_first, wide)
        l0 = coef_at(1, plane + 1, wide_first, wide)
        total = (
            0.5 * (m0 + coef_at(0, plane + 2, wide_first, wide))
            + 0.5 * (m0 + coef_at(0, plane, wide_first, wide))
            + 0.5 * (m0 + coef_at(0, plane + 1, wide_first + 1, wide))
            + 0.5 * (m0 + coef_at(0, plane + 1, wide_first - 1, wide))
            + 0.5 * (m0 + up(m0))
            + 0.5 * (m0 + down(m0))
            + l0
        )
        sides = (
            coef_at(1, plane, wide_first, wide),
            coef_at(1, plane + 1, wide_first - 1, wide),
            down(l0),
        )
        ok = row_ok
        if plane == 0:
            ok = jnp.logical_and(ok, gx > 0)
        if plane == 3:
            ok = jnp.logical_and(ok, gx < n_gx - 1)
        for c in range(3):
            inv[c, plane, wide_first : wide_first + wide, :] = jnp.where(
                ok, 1.0 / (total + sides[c]), 0.0
            )
    arrive(rhs, (), "fine", 1, ALL)
    wide_rows = slice(wide_first, wide_first + wide)
    for plane in range(4):
        for c in range(3):
            dirs[0, c, plane, wide_rows, :] = (
                steps[0][1] * inv[c, plane, wide_rows, :] * rhs[c, plane, wide_rows, :]
            )

    near_high = lax.rem(gx, 2) == 0

    def relax(k, source, target, following, round_id=None):
        for turn in range(2):
            plane = turn + 1
            if round_id is not None:
                plane = jnp.where(near_high, 2 - turn, 1 + turn)
                if turn == 0:
                    arrive(dirs, (k,), "fine", round_id, (2, 3))
                for way in (0, 1, 4, 5):
                    sx, sy = DIRS[way]
                    near = near_high if sx < 0 else jnp.logical_not(near_high)
                    now = near if turn == 0 else jnp.logical_not(near)

                    @pl.when(jnp.logical_and(now, exists(-sx, -sy)))
                    def _(way=way):
                        message(dirs, (k,), "fine", round_id, way).wait_recv()

            applied = operate(direction_load(k, H, rows), plane, H, rows)
            for c in range(3):
                left = source(c, plane) - applied[c]
                target(c, plane, left)
                if following is not None:
                    dirs[k + 1, c, plane, own, :] = (
                        following[0] * dirs[k, c, plane, own, :]
                        + following[1] * (inv[c, plane, own, :] * left)
                    )

    def into_rbuf(c, plane, value):
        rbuf[c, plane, own, :] = value

    def from_rbuf(c, plane):
        return rbuf[c, plane, own, :]

    relax(0, lambda c, plane: rhs[c, plane, own, :], into_rbuf, steps[1])
    start(dirs, (1,), "fine", 2, STAR)

    lane = lane_of(ext)
    rid = lax.broadcasted_iota(jnp.int32, (ext, lanes), 0)
    lane_even = lane % 2 == 0
    row_even = rid % 2 == 0

    def cube_sum(a):
        a = a + jnp.where(lane_even, pltpu.roll(a, lanes - 1, 1), pltpu.roll(a, 1, 1))
        return a + jnp.where(row_even, pltpu.roll(a, ext - 1, 0), pltpu.roll(a, 1, 0))

    labels = []
    label = jnp.int32(0)
    for j in range(n_gy):
        if j > 0:
            label = label + starts_ref[0, j]
        labels.append(label)
    mine = labels[0]
    before = labels[0] - 1
    after = labels[0] - 1
    for j in range(n_gy):
        mine = jnp.where(gy == j, labels[j], mine)
        if j > 0:
            before = jnp.where(gy == j, labels[j - 1], before)
        if j < n_gy - 1:
            after = jnp.where(gy == j, labels[j + 1], after)
    low_open = jnp.logical_and(gy > 0, before == mine)
    high_open = jnp.logical_and(gy < n_gy - 1, after == mine)
    inside = jnp.logical_and(
        jnp.logical_or(rid >= H, low_open), jnp.logical_or(rid < H + rows, high_open)
    )
    up2, down2 = make_zshift(ext, 2)

    def row_up(a):
        return pltpu.roll(a, ext - 2, 0)

    def row_down(a):
        return pltpu.roll(a, 2, 0)

    cmu = jnp.where(inside, 0.125 * cube_sum(coef[0, 2] + coef[0, 3]), 0.0)
    clam = jnp.where(inside, 0.125 * cube_sum(coef[1, 2] + coef[1, 3]), 0.0)
    cf = [
        0.5 * (cmu + row_up(cmu)),
        0.5 * (cmu + row_down(cmu)),
        0.5 * (cmu + up2(cmu)),
        0.5 * (cmu + down2(cmu)),
    ]
    csum = cmu + cf[0] + cf[1] + cf[2] + cf[3]
    cinv = [
        jnp.where(inside, 1.0 / (4.0 * (csum + clam + side)), 0.0)
        for side in (0.0, row_down(clam), down2(clam))
    ]

    def coarse_operate(v):
        vy_up = row_up(v[1])
        vz_up = up2(v[2])
        here = clam * ((vy_up - v[1]) + (vz_up - v[2]) - v[0])
        backs = [0.0, row_down(here), down2(here)]
        out = []
        for c in range(3):
            laplace = (
                cf[0] * ((vy_up if c == 1 else row_up(v[c])) - v[c])
                - cf[1] * (v[c] - row_down(v[c]))
                + cf[2] * ((vz_up if c == 2 else up2(v[c])) - v[c])
                - cf[3] * (v[c] - down2(v[c]))
                - cmu * v[c]
            )
            out.append(4.0 * (-laplace - (here - backs[c])))
        return out

    for c in range(3):
        for plane in (1, 2):
            sol_ref[c, plane - 1] = dirs[0, c, plane, own, :] + dirs[1, c, plane, own, :]
    relax(1, from_rbuf, into_rbuf, steps[2], 2)
    start(dirs, (2,), "fine", 3, STAR)
    for c in range(3):
        for plane in (1, 2):
            sol_ref[c, plane - 1] += dirs[2, c, plane, own, :]
    relax(2, from_rbuf, into_rbuf, None, 3)
    start(rbuf, (), "fine", 4, (2, 3, 0, 1, 4, 5, 6, 7))

    sub = lax.broadcasted_iota(jnp.int32, (8, lanes), 0)
    part = jnp.zeros((8, lanes), jnp.float32)
    for c in range(3):
        both = rbuf[c, 1, own, :] + rbuf[c, 2, own, :]
        part = jnp.where(sub == c, jnp.sum(both, axis=0, keepdims=True), part)
    sums[0] = part

    def sum_message(step):
        return pltpu.make_async_remote_copy(
            src_ref=sums.at[0],
            dst_ref=sums.at[step],
            send_sem=sum_send.at[step],
            recv_sem=sum_recv.at[step],
            device_id=(gx, lax.rem(gy + step, n_gy)),
            device_id_type=pl.DeviceIdType.MESH,
        )

    for step in range(1, n_gy):
        sum_message(step).start()

    arrive(rbuf, (), "fine", 4, (2, 3))
    left = [
        jnp.where(inside, cube_sum(rbuf[c, 1] + rbuf[c, 2]), 0.0) for c in range(3)
    ]
    coarse_steps = weights(COARSE_SWEEPS)
    direction = [coarse_steps[0][1] * cinv[c] * left[c] for c in range(3)]
    smoothed = direction
    for old, new in coarse_steps[1:]:
        applied = coarse_operate(direction)
        left = [left[c] - applied[c] for c in range(3)]
        direction = [old * direction[c] + new * (cinv[c] * left[c]) for c in range(3)]
        smoothed = [smoothed[c] + direction[c] for c in range(3)]

    total = sums[0]
    members = jnp.float32(1.0)
    for step in range(1, n_gy):
        sum_message(step).wait_recv()
        source = lax.rem(gy + n_gy - step, n_gy)
        other = labels[0]
        for j in range(1, n_gy):
            other = jnp.where(source == j, labels[j], other)
        same = jnp.where(other == mine, jnp.float32(1.0), jnp.float32(0.0))
        total = total + same * sums[step]
        members = members + same
    cells_dev = (rows // 2) * (lanes // 2)
    scale = jnp.full((8, 1), SHIFT_SCALE * cells_dev, jnp.float32) * members
    shift = jnp.sum(total, axis=1, keepdims=True) / scale
    for c in range(3):
        fc[c, 1, own, :] = smoothed[c][H : H + rows] + shift[c : c + 1, :]
    start(fc, (), "coarse", 5, ALL)
    for c in range(3):
        for plane in (1, 2):
            sol_ref[c, plane - 1] += fc[c, 1, own, :]
    arrive(rbuf, (), "fine", 4, (0, 1, 4, 5, 6, 7))
    arrive(fc, (), "coarse", 5, ALL)

    def fc_load(c, plane, dp, dy):
        return fc[c, (plane + 1 + dp) // 2, wide_first + dy : wide_first + dy + wide, :]

    for plane in range(4):
        applied = operate(fc_load, plane, wide_first, wide)
        for c in range(3):
            value = rbuf[c, plane, wide_rows, :] - applied[c]
            r2buf[c, plane, wide_rows, :] = value
            dirs[3, c, plane, wide_rows, :] = steps[0][1] * inv[c, plane, wide_rows, :] * value

    def into_r2(c, plane, value):
        r2buf[c, plane, own, :] = value

    def from_r2(c, plane):
        return r2buf[c, plane, own, :]

    def into_result(c, plane, value):
        res_ref[c, plane - 1] = value

    relax(3, from_r2, into_r2, steps[1])
    start(dirs, (4,), "fine", 6, STAR)
    for c in range(3):
        for plane in (1, 2):
            sol_ref[c, plane - 1] += dirs[3, c, plane, own, :] + dirs[4, c, plane, own, :]
    relax(4, from_r2, into_r2, steps[2], 6)
    start(dirs, (5,), "fine", 7, STAR)
    for c in range(3):
        for plane in (1, 2):
            sol_ref[c, plane - 1] += dirs[5, c, plane, own, :]
    for ref, lead, kind, round_id, way in started:

        @pl.when(exists(*DIRS[way]))
        def _(ref=ref, lead=lead, kind=kind, round_id=round_id, way=way):
            message(ref, lead, kind, round_id, way).wait_send()

    for step in range(1, n_gy):
        sum_message(step).wait_send()

    relax(5, from_r2, into_result, None, 7)


def solution(mesh):
    n_gx = mesh.shape["gx"]
    n_gy = mesh.shape["gy"]

    def shards(rhs_field, shear_modulus, lame_lambda, group_start):
        _, planes, rows, lanes = rhs_field.shape
        assert planes == 2
        ext = rows + 2 * H
        vmem = pl.BlockSpec(memory_space=pltpu.VMEM)
        hbm = pl.BlockSpec(memory_space=pltpu.MemorySpace.HBM)
        field = jax.ShapeDtypeStruct(rhs_field.shape, jnp.float32)
        f32 = jnp.float32
        return pl.pallas_call(
            functools.partial(kernel, n_gx, n_gy),
            out_shape=(field, field),
            in_specs=[hbm, hbm, hbm, hbm],
            out_specs=(vmem, vmem),
            scratch_shapes=[
                pltpu.VMEM((2, 6, ext, lanes), f32),
                pltpu.VMEM((3, 4, ext, lanes), f32),
                pltpu.VMEM((3, 4, ext, lanes), f32),
                pltpu.VMEM((6, 3, 4, ext, lanes), f32),
                pltpu.VMEM((3, 4, ext, lanes), f32),
                pltpu.VMEM((3, 4, ext, lanes), f32),
                pltpu.VMEM((3, 3, ext, lanes), f32),
                pltpu.VMEM((n_gy, 8, lanes), f32),
                pltpu.SMEM((1, n_gy), jnp.int32),
                pltpu.SemaphoreType.DMA((8, 8)),
                pltpu.SemaphoreType.DMA((8, 8)),
                pltpu.SemaphoreType.DMA((n_gy,)),
                pltpu.SemaphoreType.DMA((n_gy,)),
                pltpu.SemaphoreType.DMA((4,)),
            ],
            compiler_params=pltpu.CompilerParams(
                collective_id=0, has_side_effects=True
            ),
            cost_estimate=pl.CostEstimate(
                flops=10_000_000, bytes_accessed=400_000, transcendentals=0
            ),
        )(rhs_field, shear_modulus, lame_lambda, group_start)

    return jax.shard_map(
        shards,
        mesh=mesh,
        in_specs=(
            P(None, "gx", "gy", None),
            P("gx", "gy", None),
            P("gx", "gy", None),
            P("gx", None),
        ),
        out_specs=(P(None, "gx", "gy", None), P(None, "gx", "gy", None)),
        check_vma=False,
    )
```
